128 devices in a mesh: wide: 16 (over x, y), narrow: 8 (over z, core).
Axes of the slice: x: 4, y: 4, z: 4, core: 2. Of those that a mesh axis runs over, the one named last changes fastest.
Arguments:
- residual: bfloat16 [384, 18432], P('wide', 'narrow'), may hold values from -6 to 6
- ln_gain: float32 [18432], P('narrow'), may hold values from 0.1 to 1.9
- w_query: bfloat16 [18432, 12288], P('narrow', 'wide'), may hold values from -0.046875 to 0.046875
- w_keyval: bfloat16 [18432, 512], P('narrow', 'wide'), may hold values from -0.046875 to 0.046875
- w_out: bfloat16 [12288, 18432], P('wide', 'narrow'), may hold values from -0.0546875 to 0.0546875
- w_up: bfloat16 [18432, 36864], P('narrow', 'wide'), may hold values from -0.046875 to 0.046875
- k_cache: bfloat16 [384, 2048, 256], P('wide', 'narrow'), may hold values from -48 to 48
- v_cache: bfloat16 [384, 2048, 256], P('wide', 'narrow'), may hold values from -6 to 6
- lengths: int32 [384], P('wide'), may hold values from 1 to 2048, as said below
Outputs:
- mixed: bfloat16 [384, 18432], P('wide', 'narrow')
- scaled: bfloat16 [384, 36864], P('narrow', 'wide')
- peak: float32 [384], P('narrow')
The draws below stay inside these ranges and needn't reach their ends.
Inputs may be any that keep to these rules, and one draw needn't show every extreme that they name: `lengths`: one row has all 2048 positions filled.
All inputs are finite; a program needn't handle non-finite values. Where the reference program divides by a largest or mean magnitude, that divisor is 1e-20 or more.
Results may differ from the reference program's by a relative error of at most 0.012.
The reference program's roundings to bfloat16 on the way (of `normed`, `query`, `keyval` and `attended`) count: a program that leaves them out, or rounds other values in their place, can miss the bound.
Values may be sent and summed in bfloat16 or wider, within the bound.
No kernel may reach another device: no remote copies, remote signals or barrier semaphores. Data moves between devices by JAX's collectives and lax.ppermute only.
A program may use at most 128 MiB of HBM per device.

```python
import jax
import jax.numpy as jnp
from jax import lax

D = 18432
HEADS = 48
HEAD = 256
FF = 36864
CACHE = 2048
ROWS = 384


def draw_k_cache(key, part):
    key = jax.random.fold_in(key, 11)
    base = jnp.clip(jax.random.normal(key, (ROWS, CACHE, HEAD), jnp.float32), -6.0, 6.0)
    sign_key = jax.random.fold_in(key, 7)
    size_key = jax.random.fold_in(key, 9)
    pick_key = jax.random.fold_in(key, 13)
    signs = jnp.where(jax.random.bernoulli(sign_key, 0.5, (ROWS, CACHE, HEAD)), 1.0, -1.0)
    magnitude = jax.random.uniform(size_key, (ROWS, CACHE, HEAD), jnp.float32, 20.0, 48.0)
    hot = jax.random.bernoulli(pick_key, 0.5, (ROWS, 1, 1))
    mixed_keys = jnp.where(hot, signs * magnitude, base)
    return jnp.clip(mixed_keys, -48.0, 48.0).astype(jnp.bfloat16)


def draw_lengths(key, part):
    key = jax.random.fold_in(key, 23)
    counts = jax.random.randint(key, (ROWS,), 1, CACHE + 1, jnp.int32)
    return counts.at[0].set(CACHE)


def steps_of(stream_key, extent, shards, smallest, largest):
    def one(axis_at, parts):
        draws = jax.random.uniform(jax.random.fold_in(jax.random.fold_in(stream_key, 6), axis_at), (parts,), jnp.float32, smallest / len(shards), largest / len(shards))
        return jnp.repeat(jnp.exp(draws), extent[axis_at] // parts).reshape((-1,) + (1,) * (len(extent) - axis_at - 1))

    loudness = one(*shards[0])
    for cut in shards[1:]:
        loudness = loudness * one(*cut)
    return loudness


def gaussian(own_key, extent, spread, limit, cuts=(), held_as=jnp.bfloat16):
    entries = jax.random.normal(own_key, extent, jnp.float32) * spread
    if len(cuts) > 0:
        entries = steps_of(own_key, extent, cuts, -0.22, 0.18) * entries
    return jnp.clip(entries, min=-limit, max=limit).astype(held_as)


def setup_inputs(seed: int = 0) -> dict:
    key_of = jax.random.split(jax.random.key(seed), 10)
    return {
        "residual": gaussian(key_of[0], (ROWS, D), 1.0, 6.0, ((0, 16), (1, 8))),
        "ln_gain": jnp.clip(1.0 + 0.18 * jax.random.normal(key_of[1], (D,), jnp.float32), 0.1, 1.9),
        "w_query": gaussian(key_of[2], (D, HEADS * HEAD), D ** -0.5, 0.046875, ((0, 8), (1, 16))),
        "w_keyval": gaussian(key_of[3], (D, 2 * HEAD), D ** -0.5, 0.046875, ((0, 8), (1, 16))),
        "w_out": gaussian(key_of[4], (HEADS * HEAD, D), (HEADS * HEAD) ** -0.5, 0.0546875, ((0, 16), (1, 8))),
        "w_up": gaussian(key_of[5], (D, FF), D ** -0.5, 0.046875, ((0, 8), (1, 16))),
        "k_cache": draw_k_cache(jax.random.fold_in(key_of[9], 71), 0),
        "v_cache": gaussian(key_of[7], (ROWS, CACHE, HEAD), 1.0, 6.0, ((0, 16), (1, 8))),
        "lengths": draw_lengths(jax.random.fold_in(key_of[9], 71), 0),
    }


norm_eps = 1e-05
peak_eps = 1e-06

def reference(residual, ln_gain, w_query, w_keyval, w_out, w_up, k_cache, v_cache, lengths):
    residual_f32 = residual.astype(jnp.float32)
    mean = lax.optimization_barrier(jnp.sum(residual_f32, axis=1)) / D
    variance = lax.optimization_barrier(jnp.sum(residual_f32 * residual_f32, axis=1)) / D - mean * mean
    normed = ((residual_f32 - mean[:, None]) * lax.rsqrt(variance + norm_eps)[:, None] * ln_gain[None, :]).astype(jnp.bfloat16)
    query = jnp.dot(normed, w_query, preferred_element_type=jnp.float32).astype(jnp.bfloat16)
    query = query.reshape(ROWS, HEADS, HEAD)
    keyval = jnp.dot(normed, w_keyval, preferred_element_type=jnp.float32).astype(jnp.bfloat16)
    up = jnp.dot(normed, w_up, preferred_element_type=jnp.float32)
    factor = 1.0 / HEAD ** 0.5

    def one_row(items):
        q_row, k_rows, v_rows, kv_row, count = items
        scores = jnp.dot(q_row, k_rows.T, preferred_element_type=jnp.float32) * factor
        valid = jnp.arange(CACHE, dtype=jnp.int32) < count
        masked = jnp.where(valid[None, :], scores, jnp.float32(-1e+30))
        top = lax.optimization_barrier(jnp.max(masked, axis=1))
        probs = jnp.where(valid[None, :], jnp.exp(masked - top[:, None]), jnp.float32(0.0))
        total = lax.optimization_barrier(jnp.sum(probs, axis=1))
        partial_value = jnp.dot(probs.astype(jnp.bfloat16), v_rows, preferred_element_type=jnp.float32)
        own = jnp.dot(q_row, kv_row[:HEAD], preferred_element_type=jnp.float32) * factor
        both = jnp.maximum(top, own)
        keep = jnp.exp(top - both)
        fresh = jnp.exp(own - both)
        mass = total * keep + fresh
        fresh_b = lax.optimization_barrier(fresh.astype(jnp.bfloat16))
        new_term = fresh_b.astype(jnp.float32)[:, None] * kv_row[HEAD:].astype(jnp.float32)[None, :]
        result = (partial_value * keep[:, None] + new_term) / mass[:, None]
        return result.astype(jnp.bfloat16).reshape(HEADS * HEAD)
    attended = lax.map(one_row, (query, k_cache, v_cache, keyval, lengths))
    mixed = (residual_f32 + jnp.dot(attended, w_out, preferred_element_type=jnp.float32)).astype(jnp.bfloat16)
    peak = lax.optimization_barrier(jnp.max(jnp.abs(up), axis=1))
    scaled = (up / (peak + peak_eps)[:, None]).astype(jnp.bfloat16)
    return (mixed, scaled, peak)
```

```python
import functools

import jax
import jax.numpy as jnp
from jax import lax
from jax.experimental import pallas as pl
from jax.experimental.pallas import tpu as pltpu
from jax.sharding import PartitionSpec as P

D = 18432
HEADS = 48
HEAD = 256
WIDE = 16
NARROW = 8
RING = 4
ROWS = 384
LOCAL = ROWS // WIDE
EACH = LOCAL // NARROW
QCOLS = HEADS * HEAD // WIDE
HELD = QCOLS // HEAD
KVCOLS = 2 * HEAD // WIDE
HCOLS = QCOLS + 128
PACK = HEAD + 128
FEATS = D // NARROW
SHARE = ROWS // NARROW
UPCOLS = 36864 // WIDE

norm_eps = 1e-05
peak_eps = 1e-06

f32, bf16 = jnp.float32, jnp.bfloat16
SAME_CORE = [[w * NARROW + z * 2 + c for w in range(WIDE) for z in range(RING)] for c in range(2)]


def swap_core(x):
    return lax.ppermute(x, "narrow", [(i, i ^ 1) for i in range(NARROW)])


def shift_z(x, by):
    return lax.ppermute(x, "narrow", [(i, ((i // 2 + by) % RING) * 2 + i % 2) for i in range(NARROW)])


def spread(x):
    x = jnp.broadcast_to(x[:, None], (WIDE, RING) + x.shape[1:]).reshape((WIDE * RING,) + x.shape[1:])
    return lax.all_to_all(x, ("wide", "narrow"), 0, 0, axis_index_groups=SAME_CORE, tiled=True)


def dot(a, b):
    return jnp.dot(a, b, preferred_element_type=f32)


def full(shape):
    return pl.BlockSpec(shape, lambda *_: (0,) * len(shape))


def params(mib):
    return pltpu.CompilerParams(vmem_limit_bytes=mib * 1024 * 1024)


def cost(flops, moved):
    return pl.CostEstimate(flops=int(flops), bytes_accessed=int(moved), transcendentals=0)


def head_kernel(place, x_ref, wq_ref, wkv_ref, keep_ref, send_ref, acc_ref):
    z, c = place[0], place[1]
    tile = wq_ref.shape[1]

    def deal(terms, first):
        for lanes in range(terms.shape[1] // 128):
            acc_ref[lanes] = terms[:, lanes * 128 : (lanes + 1) * 128]
        for n in range(NARROW):
            at = lax.rem(n // 2 - z + RING, RING)
            for lanes in range(terms.shape[1] // 128):
                rows = acc_ref[lanes, pl.ds(n, SHARE, stride=NARROW), :]
                columns = pl.ds(pl.multiple_of(first + lanes * 128, 128), 128)

                @pl.when(c == n % 2)
                def _():
                    keep_ref[at, :, columns] = rows

                @pl.when(c != n % 2)
                def _():
                    send_ref[at, :, columns] = rows

    step = pl.program_id(0)
    deal(dot(x_ref[...], wq_ref[...]), step * tile)

    @pl.when(step == 0)
    def _():
        deal(jnp.concatenate([dot(x_ref[...], wkv_ref[...]), jnp.zeros((ROWS, 128 - KVCOLS), f32)], axis=1), QCOLS)


def head_terms(place, x, w_query, w_keyval):
    tile = 256
    out = jax.ShapeDtypeStruct((RING, SHARE, HCOLS), f32)
    return pl.pallas_call(
        head_kernel,
        grid_spec=pltpu.PrefetchScalarGridSpec(
            num_scalar_prefetch=1,
            grid=(QCOLS // tile,),
            in_specs=[
                full((ROWS, FEATS)),
                pl.BlockSpec((FEATS, tile), lambda i, _: (0, i)),
                full((FEATS, KVCOLS)),
            ],
            out_specs=[full(out.shape), full(out.shape)],
            scratch_shapes=[pltpu.VMEM((tile // 128, ROWS, 128), f32)],
        ),
        out_shape=[out, out],
        compiler_params=params(32),
        cost_estimate=cost(2 * ROWS * FEATS * (QCOLS + KVCOLS), 2 * FEATS * (ROWS + QCOLS + 128) + 8 * out.size),
    )(place, x, w_query, w_keyval)


def up_kernel(x_ref, w_ref, out_ref):
    out_ref[...] = dot(x_ref[...], w_ref[...]).astype(bf16)


def up_terms(x, w_up):
    tile = 384
    return pl.pallas_call(
        up_kernel,
        grid=(UPCOLS // tile,),
        in_specs=[full((ROWS, FEATS)), pl.BlockSpec((FEATS, tile), lambda i: (0, i))],
        out_specs=pl.BlockSpec((ROWS, tile), lambda i: (0, i)),
        out_shape=jax.ShapeDtypeStruct((ROWS, UPCOLS), bf16),
        compiler_params=params(32),
        cost_estimate=cost(2 * ROWS * FEATS * UPCOLS, 2 * (FEATS * (ROWS + UPCOLS) + ROWS * UPCOLS)),
    )(x, w_up)


def parts(value):
    high = value.astype(bf16).astype(f32)
    rest = value - high
    middle = rest.astype(bf16).astype(f32)
    return high, middle, (rest - middle).astype(bf16).astype(f32)


def packed(top, total):
    lane = lax.broadcasted_iota(jnp.int32, (top.shape[0], 128), 1)
    out = jnp.zeros(lane.shape, f32)
    for at, part in enumerate(parts(top) + parts(total)):
        out = jnp.where(lane == at, part, out)
    return out.astype(bf16)


def unpacked(block):
    held = block[:, HEAD:PACK].astype(f32)
    top = held[:, 0:1] + held[:, 1:2] + held[:, 2:3]
    total = held[:, 3:4] + held[:, 4:5] + held[:, 5:6]
    return block[:, :HEAD].astype(f32), top, total


def group_of(step, place):
    return lax.rem(place[0] + lax.rem(step, RING), RING) * 2 + (place[1] + step // RING) % 2


def chosen(rows, columns, source):
    made = lax.broadcasted_iota(jnp.int32, (rows, columns), 0)
    held = lax.broadcasted_iota(jnp.int32, (rows, columns), 1)
    return jnp.where(source(made) == held, 1.0, 0.0).astype(bf16)


def by_row(block):
    return dot(chosen(SHARE, SHARE, lambda i: lax.rem(i, WIDE) * EACH + i // WIDE), block)


def heads_of(rows):
    return jnp.concatenate([rows[:, h * HEAD : (h + 1) * HEAD] for h in range(HELD)], axis=0)


def attend_kernel(place, lengths, q_ref, k_ref, v_ref, keep_ref, send_ref):
    step = pl.program_id(0)
    group = group_of(step, place)
    start = (place[0] * 2 + place[1]) * k_ref.shape[2]
    rows = by_row(q_ref[0])
    for j in range(EACH):
        query = heads_of(rows[j * WIDE : (j + 1) * WIDE]).astype(bf16)
        scores = lax.dot_general(query, k_ref[j, 0], (((1,), (1,)), ((), ())), preferred_element_type=f32)
        scores = scores * (1.0 / HEAD**0.5)
        position = lax.broadcasted_iota(jnp.int32, scores.shape, 1) + start
        valid = position < lengths[j * NARROW + group]
        masked = jnp.where(valid, scores, f32(-1e30))
        top = jnp.max(masked, axis=1, keepdims=True)
        probs = jnp.where(valid, jnp.exp(masked - top), f32(0.0))
        total = jnp.sum(probs, axis=1, keepdims=True)
        value = dot(probs.astype(bf16), v_ref[j, 0]).astype(bf16)
        block = jnp.concatenate([value, packed(top, total)], axis=1)
        span = slice(j * HEADS, (j + 1) * HEADS)

        @pl.when(step < RING)
        def _():
            keep_ref[lax.rem(step, RING), span, :] = block

        @pl.when(step >= RING)
        def _():
            send_ref[lax.rem(step, RING), span, :] = block


def attend(place, lengths, query, k_cache, v_cache):
    positions = k_cache.shape[1]
    k_cache = k_cache.reshape(EACH, NARROW, positions, HEAD)
    v_cache = v_cache.reshape(EACH, NARROW, positions, HEAD)
    cache = pl.BlockSpec((EACH, 1, positions, HEAD), lambda i, place, _: (0, group_of(i, place), 0, 0))
    out = jax.ShapeDtypeStruct((RING, EACH * HEADS, PACK), bf16)
    return pl.pallas_call(
        attend_kernel,
        grid_spec=pltpu.PrefetchScalarGridSpec(
            num_scalar_prefetch=2,
            grid=(NARROW,),
            in_specs=[
                pl.BlockSpec(
                    (1, SHARE, HCOLS),
                    lambda i, place, _: ((i // RING) * RING + lax.rem(place[0] + lax.rem(i, RING), RING), 0, 0),
                ),
                cache,
                cache,
            ],
            out_specs=[full(out.shape), full(out.shape)],
        ),
        out_shape=[out, out],
        compiler_params=params(32),
        cost_estimate=cost(4 * LOCAL * HEADS * positions * HEAD, 4 * k_cache.size + 4 * out.size + 2 * query.size),
    )(place, lengths, query, k_cache, v_cache)


def joined(first, second):
    value_a, top_a, total_a = first
    value_b, top_b, total_b = second
    both = jnp.maximum(top_a, top_b)
    keep_a = jnp.exp(top_a - both)
    keep_b = jnp.exp(top_b - both)
    return value_a * keep_a + value_b * keep_b, both, total_a * keep_a + total_b * keep_b


def pair_kernel(a_ref, b_ref, *out_refs):
    for at, out_ref in enumerate(out_refs):
        value, top, total = joined(unpacked(a_ref[at]), unpacked(b_ref[at]))
        out_ref[...] = jnp.concatenate([value.astype(bf16), packed(top, total)], axis=1)


def pair(a, b):
    out = jax.ShapeDtypeStruct(a.shape[1:], bf16)
    return pl.pallas_call(
        pair_kernel,
        out_shape=[out] * RING,
        compiler_params=params(32),
        cost_estimate=cost(4 * a.size, 6 * a.size),
    )(a, b)


def row_of(block):
    spot = lax.broadcasted_iota(jnp.int32, (KVCOLS, HEAD), 0)
    lane = lax.broadcasted_iota(jnp.int32, (KVCOLS, HEAD), 1)
    tiled = dot(block, (lax.rem(lane, KVCOLS) == spot).astype(bf16))
    row = lax.broadcasted_iota(jnp.int32, tiled.shape, 0)
    lane = lax.broadcasted_iota(jnp.int32, tiled.shape, 1)
    return jnp.sum(jnp.where(lane // KVCOLS == row, tiled, 0.0), axis=0, keepdims=True)


def finish_kernel(q_ref, peak_ref, *refs):
    blocks, out_ref = refs[:RING], refs[RING]
    rows = by_row(q_ref[...])
    made = []
    for j in range(EACH):
        mine = rows[j * WIDE : (j + 1) * WIDE]
        query = heads_of(mine)
        keyval = mine[:, QCOLS : QCOLS + KVCOLS].astype(bf16)
        new_key = row_of(keyval[: WIDE // 2])
        new_value = row_of(keyval[WIDE // 2 :])
        own = jnp.sum(query * new_key, axis=1, keepdims=True) * (1.0 / HEAD**0.5)
        span = slice(j * HEADS, (j + 1) * HEADS)
        value, top, total = functools.reduce(joined, [unpacked(ref[span, :]) for ref in blocks])
        both = jnp.maximum(top, own)
        keep = jnp.exp(top - both)
        fresh = jnp.exp(own - both)
        mass = total * keep + fresh
        done = ((value * keep + fresh.astype(bf16).astype(f32) * new_value) / mass).astype(bf16)
        made.append(jnp.concatenate([done[h * WIDE : (h + 1) * WIDE] for h in range(HELD)], axis=1))
    each = EACH + 1
    order = chosen(WIDE * each, SHARE, lambda i: jnp.where(lax.rem(i, each) < EACH, lax.rem(i, each) * WIDE + i // each, -1))
    made = dot(order, jnp.concatenate(made, axis=0))
    peaks = jnp.concatenate(parts(peak_ref[...]) + (jnp.zeros((1, QCOLS - 3 * 128), f32),), axis=1)
    row = lax.broadcasted_iota(jnp.int32, made.shape, 0)
    out_ref[...] = jnp.where(lax.rem(row, each) == EACH, peaks, made).astype(bf16)


def finish(query, peak, blocks):
    out = (WIDE * (EACH + 1), QCOLS)
    return pl.pallas_call(
        finish_kernel,
        out_shape=jax.ShapeDtypeStruct(out, bf16),
        compiler_params=params(32),
        cost_estimate=cost(40 * blocks[0].size, 10 * blocks[0].size),
    )(query, peak, *blocks)


def out_kernel(place, own_ref, other_ref, w_ref, out_ref, rows_ref):
    @pl.when(pl.program_id(0) == 0)
    def _():
        shape = (ROWS, own_ref.shape[0])
        made = lax.broadcasted_iota(jnp.int32, shape, 0)
        held = lax.broadcasted_iota(jnp.int32, shape, 1)
        local = lax.rem(made, LOCAL)
        group = lax.rem(local, NARROW)
        source = ((made // LOCAL) * RING + group // 2) * (EACH + 1) + local // NARROW
        total = jnp.zeros((ROWS, QCOLS), f32)
        for core, ref in ((place[1], own_ref), (1 - place[1], other_ref)):
            pick = jnp.where(source == held, jnp.where(lax.rem(group, 2) == core, 1.0, 0.0), 0.0)
            total += dot(pick.astype(bf16), ref[...])
        rows_ref[...] = total.astype(bf16)

    out_ref[...] = dot(rows_ref[...], w_ref[...]).astype(bf16)


def out_terms(place, own, other, w_out):
    tile = 384
    return pl.pallas_call(
        out_kernel,
        grid_spec=pltpu.PrefetchScalarGridSpec(
            num_scalar_prefetch=1,
            grid=(FEATS // tile,),
            in_specs=[full(own.shape), full(own.shape), pl.BlockSpec((QCOLS, tile), lambda i, _: (0, i))],
            out_specs=pl.BlockSpec((ROWS, tile), lambda i, _: (0, i)),
            scratch_shapes=[pltpu.VMEM((ROWS, QCOLS), bf16)],
        ),
        out_shape=jax.ShapeDtypeStruct((ROWS, FEATS), bf16),
        compiler_params=params(32),
        cost_estimate=cost(2 * ROWS * QCOLS * FEATS, 2 * (QCOLS * FEATS + ROWS * FEATS)),
    )(place, own, other, w_out)


def shards(residual, ln_gain, w_query, w_keyval, w_out, w_up, k_cache, v_cache, lengths):
    narrow = lax.axis_index("narrow")
    place = jnp.stack([narrow // 2, narrow % 2]).astype(jnp.int32)
    residual_f32 = residual.astype(f32)
    sums = jnp.stack([jnp.sum(residual_f32, axis=1), jnp.sum(residual_f32 * residual_f32, axis=1)])
    sums = sums + swap_core(sums)
    sums = sums + shift_z(sums, 1) + shift_z(sums, 2) + shift_z(sums, 3)
    mean = sums[0] / D
    variance = sums[1] / D - mean * mean
    normed = (
        (residual_f32 - mean[:, None]) * lax.rsqrt(variance + norm_eps)[:, None] * ln_gain[None, :]
    ).astype(bf16)
    rows = lax.all_to_all(jnp.broadcast_to(normed[None], (WIDE,) + normed.shape), "wide", 0, 0, tiled=True)
    rows = rows.reshape(ROWS, FEATS)

    keep, send = head_terms(place, rows, w_query, w_keyval)
    both = keep + swap_core(send)
    query = (both[0] + shift_z(both[1], 1) + shift_z(both[2], 2) + shift_z(both[3], 3)).astype(bf16)

    up = lax.psum_scatter(up_terms(rows, w_up), "narrow", scatter_dimension=0, tiled=True).astype(f32)
    peak = jnp.max(jnp.abs(up), axis=1)

    query = spread(query.reshape(WIDE, EACH, HCOLS)).reshape(WIDE, RING, EACH, HCOLS)
    query = query.transpose(1, 0, 2, 3).reshape(RING, SHARE, HCOLS)
    query = jnp.concatenate([query, swap_core(query)])
    keep, send = attend(place, lengths, query, k_cache, v_cache)
    blocks = pair(keep, swap_core(send))
    blocks = [blocks[0]] + [shift_z(blocks[d], d) for d in range(1, RING)]
    mine = lax.dynamic_index_in_dim(query, place[0], keepdims=False)
    attended = finish(mine, jnp.pad(peak, (0, 128 - SHARE))[None], blocks)

    own = spread(attended.reshape(WIDE, EACH + 1, QCOLS))
    peaks = lax.dynamic_index_in_dim(own.reshape(WIDE, RING, EACH + 1, QCOLS)[:, :, EACH], place[0], 1, keepdims=False)
    peaks = peaks.astype(f32)
    peaks = peaks[:, :SHARE] + peaks[:, 128 : 128 + SHARE] + peaks[:, 256 : 256 + SHARE]
    peak = jnp.max(peaks, axis=0)
    own = own.reshape(WIDE * RING * (EACH + 1), QCOLS)
    projected = out_terms(place, own, swap_core(own), w_out)
    projected = lax.all_to_all(projected.reshape(WIDE, LOCAL, FEATS), "wide", 0, 0, tiled=True)
    mixed = (residual_f32 + jnp.sum(projected.astype(f32), axis=0)).astype(bf16)
    scaled = (up / (peak + peak_eps)[:, None]).astype(bf16)
    return (mixed, scaled, peak)


def solution(mesh):
    placed = (
        P("wide", "narrow"),
        P("narrow"),
        P("narrow", "wide"),
        P("narrow", "wide"),
        P("wide", "narrow"),
        P("narrow", "wide"),
        P("wide", "narrow", None),
        P("wide", "narrow", None),
        P("wide"),
    )
    return jax.shard_map(
        shards,
        mesh=mesh,
        in_specs=placed,
        out_specs=(P("wide", "narrow"), P("narrow", "wide"), P("narrow")),
        check_vma=False,
    )
```

```python
import functools

import jax
import jax.numpy as jnp
from jax import lax
from jax.experimental import pallas as pl
from jax.experimental.pallas import tpu as pltpu
from jax.sharding import PartitionSpec as P

D = 18432
HEADS = 48
HEAD = 256
WIDE = 16
NARROW = 8
RING = 4
ROWS = 384
LOCAL = ROWS // WIDE
EACH = LOCAL // NARROW
QCOLS = HEADS * HEAD // WIDE
HELD = QCOLS // HEAD
KVCOLS = 2 * HEAD // WIDE
HCOLS = QCOLS + 128
PACK = HEAD + 128
FEATS = D // NARROW
SHARE = ROWS // NARROW
UPCOLS = 36864 // WIDE
HALF = FEATS // 2

norm_eps = 1e-05
peak_eps = 1e-06

f32, bf16 = jnp.float32, jnp.bfloat16
SAME_CORE = [[w * NARROW + z * 2 + c for w in range(WIDE) for z in range(RING)] for c in range(2)]


def swap_core(x):
    return lax.ppermute(x, "narrow", [(i, i ^ 1) for i in range(NARROW)])


def shift_z(x, by):
    return lax.ppermute(x, "narrow", [(i, ((i // 2 + by) % RING) * 2 + i % 2) for i in range(NARROW)])


def shift_x(x, by):
    return lax.ppermute(x, "wide", [(i, ((i // RING + by) % RING) * RING + i % RING) for i in range(WIDE)])


def shift_y(x, by):
    return lax.ppermute(x, "wide", [(i, (i // RING) * RING + (i + by) % RING) for i in range(WIDE)])


def gathered(normed):
    left, right = normed[:, :HALF], normed[:, HALF:]
    left = jnp.concatenate([left] + [shift_x(left, by) for by in range(1, RING)])
    right = jnp.concatenate([right] + [shift_y(right, by) for by in range(1, RING)])
    return (
        [left] + [shift_y(left, by) for by in range(1, RING)],
        [right] + [shift_x(right, by) for by in range(1, RING)],
    )


def spread(x):
    x = jnp.broadcast_to(x[:, None], (WIDE, RING) + x.shape[1:]).reshape((WIDE * RING,) + x.shape[1:])
    return lax.all_to_all(x, ("wide", "narrow"), 0, 0, axis_index_groups=SAME_CORE, tiled=True)


def dot(a, b):
    return jnp.dot(a, b, preferred_element_type=f32)


def full(shape):
    return pl.BlockSpec(shape, lambda *_: (0,) * len(shape))


def params(mib):
    return pltpu.CompilerParams(vmem_limit_bytes=mib * 1024 * 1024)


def cost(flops, moved):
    return pl.CostEstimate(flops=int(flops), bytes_accessed=int(moved), transcendentals=0)


WHOLE = pl.BlockSpec(memory_space=pltpu.VMEM)


def slot_of(wide, z, c):
    to_z, to_c = lax.rem((wide >> 2) - z + RING, RING), (wide >> 1) & 1
    return ((to_c ^ c) * RING + to_z) * 2 + (wide & 1)


def held_in(slot, z, c):
    to_z, to_c = lax.rem((slot >> 1) % RING + z, RING), (slot >> 3) ^ c
    return (to_z * 2 + to_c) * 2 + (slot & 1)


def head_kernel(place, *refs):
    left, right = refs[:RING], refs[RING : 2 * RING]
    wq_ref, wkv_ref, keep_ref, send_ref, x_ref, acc_ref, rows_ref = refs[2 * RING :]
    z, c, x, y = place[0], place[1], place[2], place[3]
    for outer in range(RING):
        for first, ref in ((0, left[outer]), (HALF, right[outer])):
            held = ref[...].astype(f32)
            for inner in range(RING):
                by_x, by_y = (inner, outer) if first == 0 else (outer, inner)
                source = lax.rem(x - by_x + RING, RING) * RING + lax.rem(y - by_y + RING, RING)
                at = pl.ds(pl.multiple_of(slot_of(source, z, c) * LOCAL, 8), LOCAL)
                rows_ref[at, first : first + HALF] = held[inner * LOCAL : (inner + 1) * LOCAL]
    x_ref[...] = rows_ref[...].astype(bf16)

    def deal(terms, first):
        for at in range(WIDE):
            rows = pl.ds(pl.multiple_of(held_in(at, z, c) * LOCAL, 8), LOCAL)
            for lanes in range(terms.shape[1] // 128):
                acc_ref[lanes, rows, :] = terms[at * LOCAL : (at + 1) * LOCAL, lanes * 128 : (lanes + 1) * 128]
        for n in range(NARROW):
            at = lax.rem(n // 2 - z + RING, RING)
            for lanes in range(terms.shape[1] // 128):
                rows = acc_ref[lanes, pl.ds(n, SHARE, stride=NARROW), :]
                columns = slice(first + lanes * 128, first + (lanes + 1) * 128)

                @pl.when(c == n % 2)
                def _():
                    keep_ref[at, :, columns] = rows

                @pl.when(c != n % 2)
                def _():
                    send_ref[at, :, columns] = rows

    for first in range(0, QCOLS, 256):
        deal(dot(x_ref[...], wq_ref[:, first : first + 256]), first)
    deal(jnp.concatenate([dot(x_ref[...], wkv_ref[...]), jnp.zeros((ROWS, 128 - KVCOLS), f32)], axis=1), QCOLS)


def head_terms(place, left, right, w_query, w_keyval):
    out = jax.ShapeDtypeStruct((RING, SHARE, HCOLS), f32)
    rows = jax.ShapeDtypeStruct((ROWS, FEATS), bf16)
    return pl.pallas_call(
        head_kernel,
        grid_spec=pltpu.PrefetchScalarGridSpec(
            num_scalar_prefetch=1,
            grid=(1,),
            in_specs=[WHOLE] * (2 * RING + 2),
            out_specs=[WHOLE] * 3,
            scratch_shapes=[pltpu.VMEM((2, ROWS, 128), f32), pltpu.VMEM((ROWS, FEATS), f32)],
        ),
        out_shape=[out, out, rows],
        compiler_params=params(20),
        cost_estimate=cost(2 * ROWS * FEATS * (QCOLS + KVCOLS), 2 * FEATS * (ROWS + QCOLS + 128) + 8 * out.size),
    )(place, *left, *right, w_query, w_keyval)


def up_kernel(x_ref, w_ref, keep_ref, send_ref):
    half = ROWS // 2
    terms = dot(x_ref[...], w_ref[...]).astype(bf16)
    for at in range(RING):
        keep_ref[at] = terms[at * SHARE : (at + 1) * SHARE]
        send_ref[at] = terms[half + at * SHARE : half + (at + 1) * SHARE]


def up_terms(x, w_up):
    tile = 768
    out = jax.ShapeDtypeStruct((RING, SHARE, UPCOLS), bf16)
    block = pl.BlockSpec((RING, SHARE, tile), lambda i: (0, 0, i))
    return pl.pallas_call(
        up_kernel,
        grid=(UPCOLS // tile,),
        in_specs=[full((ROWS, FEATS)), pl.BlockSpec((FEATS, tile), lambda i: (0, i))],
        out_specs=[block, block],
        out_shape=[out, out],
        compiler_params=params(16),
        cost_estimate=cost(2 * ROWS * FEATS * UPCOLS, 2 * (FEATS * (ROWS + UPCOLS) + ROWS * UPCOLS)),
    )(x, w_up)


def parts(value):
    high = value.astype(bf16).astype(f32)
    rest = value - high
    middle = rest.astype(bf16).astype(f32)
    return high, middle, (rest - middle).astype(bf16).astype(f32)


def packed(top, total):
    lane = lax.broadcasted_iota(jnp.int32, (top.shape[0], 128), 1)
    out = jnp.zeros(lane.shape, f32)
    for at, part in enumerate(parts(top) + parts(total)):
        out = jnp.where(lane == at, part, out)
    return out.astype(bf16)


def unpacked(block):
    held = block[:, HEAD:PACK].astype(f32)
    top = held[:, 0:1] + held[:, 1:2] + held[:, 2:3]
    total = held[:, 3:4] + held[:, 4:5] + held[:, 5:6]
    return block[:, :HEAD].astype(f32), top, total


def chosen(rows, columns, source):
    made = lax.broadcasted_iota(jnp.int32, (rows, columns), 0)
    held = lax.broadcasted_iota(jnp.int32, (rows, columns), 1)
    return jnp.where(source(made) == held, 1.0, 0.0).astype(bf16)


def by_row(block):
    return dot(chosen(SHARE, SHARE, lambda i: lax.rem(i, WIDE) * EACH + i // WIDE), block)


def heads_of(rows):
    return jnp.concatenate([rows[:, h * HEAD : (h + 1) * HEAD] for h in range(HELD)], axis=0)


def attend_kernel(away, place, lengths, q_ref, k_ref, v_ref, out_ref):
    group = group_of(away, pl.program_id(0), place)
    positions = k_ref.shape[2]
    start = (place[0] * 2 + place[1]) * positions
    rows = by_row(q_ref[0])
    position = lax.broadcasted_iota(jnp.int32, (HEADS, positions), 1) + start
    valid = jnp.concatenate([position < lengths[j * NARROW + group] for j in range(EACH)], axis=0)
    scores = jnp.concatenate(
        [
            lax.dot_general(
                heads_of(rows[j * WIDE : (j + 1) * WIDE]).astype(bf16),
                k_ref[j, 0],
                (((1,), (1,)), ((), ())),
                preferred_element_type=f32,
            )
            for j in range(EACH)
        ],
        axis=0,
    )
    masked = jnp.where(valid, scores * (1.0 / HEAD**0.5), f32(-1e30))
    top = jnp.max(masked, axis=1, keepdims=True)
    probs = jnp.where(valid, jnp.exp(masked - top), f32(0.0))
    total = jnp.sum(probs, axis=1, keepdims=True)
    weights = probs.astype(bf16)
    for j in range(EACH):
        span = slice(j * HEADS, (j + 1) * HEADS)
        out_ref[0, span, :HEAD] = dot(weights[span], v_ref[j, 0]).astype(bf16)
    out_ref[0, :, HEAD:] = packed(top, total)


def group_of(away, step, place):
    at = lax.rem(place[0] + step, RING) * 2
    return at + (1 - place[1] if away else place[1])


def attend(away, place, lengths, query, k_cache, v_cache):
    positions = k_cache.shape[1]
    k_cache = k_cache.reshape(EACH, NARROW, positions, HEAD)
    v_cache = v_cache.reshape(EACH, NARROW, positions, HEAD)
    cache = pl.BlockSpec((EACH, 1, positions, HEAD), lambda i, place, _: (0, group_of(away, i, place), 0, 0))
    out = jax.ShapeDtypeStruct((RING, EACH * HEADS, PACK), bf16)
    return pl.pallas_call(
        functools.partial(attend_kernel, away),
        grid_spec=pltpu.PrefetchScalarGridSpec(
            num_scalar_prefetch=2,
            grid=(RING,),
            in_specs=[
                pl.BlockSpec((1, SHARE, HCOLS), lambda i, place, _: (lax.rem(place[0] + i, RING), 0, 0)),
                cache,
                cache,
            ],
            out_specs=pl.BlockSpec((1, EACH * HEADS, PACK), lambda i, *_: (i, 0, 0)),
        ),
        out_shape=out,
        compiler_params=params(6),
        cost_estimate=cost(2 * LOCAL * HEADS * positions * HEAD, 2 * k_cache.size + 2 * out.size + 2 * query.size),
    )(place, lengths, query, k_cache, v_cache)


def joined(first, second):
    value_a, top_a, total_a = first
    value_b, top_b, total_b = second
    both = jnp.maximum(top_a, top_b)
    keep_a = jnp.exp(top_a - both)
    keep_b = jnp.exp(top_b - both)
    return value_a * keep_a + value_b * keep_b, both, total_a * keep_a + total_b * keep_b


def pair_kernel(a_ref, b_ref, up_a_ref, up_b_ref, own_ref, up_ref, *send_refs):
    for at in range(RING):
        value, top, total = joined(unpacked(a_ref[at]), unpacked(b_ref[at]))
        block = jnp.concatenate([value.astype(bf16), packed(top, total)], axis=1)
        up = up_a_ref[at].astype(f32) + up_b_ref[at].astype(f32)
        if at == 0:
            own_ref[...] = block
            up_ref[...] = up
        else:
            ref = send_refs[at - 1]
            for j in range(EACH):
                ref[:, j * PACK : (j + 1) * PACK] = block[j * HEADS : (j + 1) * HEADS]
            ref[:, EACH * PACK :] = up.astype(bf16)


def pair(a, b, up_a, up_b):
    out = [jax.ShapeDtypeStruct(a.shape[1:], bf16), jax.ShapeDtypeStruct(up_a.shape[1:], f32)]
    out += [jax.ShapeDtypeStruct((SHARE, EACH * PACK + UPCOLS), bf16)] * (RING - 1)
    return pl.pallas_call(
        pair_kernel,
        out_shape=out,
        compiler_params=params(12),
        cost_estimate=cost(4 * a.size, 6 * a.size + 6 * up_a.size),
    )(a, b, up_a, up_b)


def row_of(block):
    spot = lax.broadcasted_iota(jnp.int32, (KVCOLS, HEAD), 0)
    lane = lax.broadcasted_iota(jnp.int32, (KVCOLS, HEAD), 1)
    tiled = dot(block, (lax.rem(lane, KVCOLS) == spot).astype(bf16))
    row = lax.broadcasted_iota(jnp.int32, tiled.shape, 0)
    lane = lax.broadcasted_iota(jnp.int32, tiled.shape, 1)
    return jnp.sum(jnp.where(lane // KVCOLS == row, tiled, 0.0), axis=0, keepdims=True)


def finish_kernel(place, q_ref, own_ref, up_own_ref, *refs):
    blocks, (out_ref, up_ref) = refs[: RING - 1], refs[RING - 1 :]
    up = sum((ref[:, EACH * PACK :].astype(f32) for ref in blocks), up_own_ref[...])
    up_ref[...] = up
    rows = by_row(q_ref[place[0]])
    made = []
    for j in range(EACH):
        mine = rows[j * WIDE : (j + 1) * WIDE]
        query = heads_of(mine)
        keyval = mine[:, QCOLS : QCOLS + KVCOLS].astype(bf16)
        new_key = row_of(keyval[: WIDE // 2])
        new_value = row_of(keyval[WIDE // 2 :])
        own = jnp.sum(query * new_key, axis=1, keepdims=True) * (1.0 / HEAD**0.5)
        span = slice(j * HEADS, (j + 1) * HEADS)
        held = [own_ref[span, :]] + [ref[:, j * PACK : (j + 1) * PACK] for ref in blocks]
        value, top, total = functools.reduce(joined, [unpacked(block) for block in held])
        both = jnp.maximum(top, own)
        keep = jnp.exp(top - both)
        fresh = jnp.exp(own - both)
        mass = total * keep + fresh
        done = ((value * keep + fresh.astype(bf16).astype(f32) * new_value) / mass).astype(bf16)
        made.append(jnp.concatenate([done[h * WIDE : (h + 1) * WIDE] for h in range(HELD)], axis=1))
    each = EACH + 1
    order = chosen(WIDE * each, SHARE, lambda i: jnp.where(lax.rem(i, each) < EACH, lax.rem(i, each) * WIDE + i // each, -1))
    made = dot(order, jnp.concatenate(made, axis=0))
    column = jnp.max(jnp.abs(up), axis=1, keepdims=True)
    row = lax.broadcasted_iota(jnp.int32, (SHARE, 128), 0)
    lane = lax.broadcasted_iota(jnp.int32, (SHARE, 128), 1)
    peak = jnp.sum(jnp.where(row == lane, column, 0.0), axis=0, keepdims=True)
    peaks = jnp.concatenate(parts(peak) + (jnp.zeros((1, QCOLS - 3 * 128), f32),), axis=1)
    row = lax.broadcasted_iota(jnp.int32, made.shape, 0)
    out_ref[...] = jnp.where(lax.rem(row, each) == EACH, peaks, made).astype(bf16)


def finish(place, query, own, up_own, blocks):
    out = [
        jax.ShapeDtypeStruct((WIDE * (EACH + 1), QCOLS), bf16),
        jax.ShapeDtypeStruct(up_own.shape, f32),
    ]
    return pl.pallas_call(
        finish_kernel,
        grid_spec=pltpu.PrefetchScalarGridSpec(
            num_scalar_prefetch=1,
            grid=(1,),
            in_specs=[WHOLE] * (len(blocks) + 3),
            out_specs=[WHOLE] * 2,
        ),
        out_shape=out,
        compiler_params=params(12),
        cost_estimate=cost(40 * own.size, 10 * own.size + 14 * up_own.size),
    )(place, query, own, up_own, *blocks)


def out_kernel(place, own_ref, other_ref, w_ref, out_ref, peak_ref):
    each = EACH + 1
    shape = (ROWS, own_ref.shape[0])
    made = lax.broadcasted_iota(jnp.int32, shape, 0)
    held = lax.broadcasted_iota(jnp.int32, shape, 1)
    local = lax.rem(made, LOCAL)
    group = lax.rem(local, NARROW)
    source = ((made // LOCAL) * RING + group // 2) * each + local // NARROW
    rows = jnp.zeros((ROWS, QCOLS), f32)
    for core, ref in ((place[1], own_ref), (1 - place[1], other_ref)):
        pick = jnp.where(source == held, jnp.where(lax.rem(group, 2) == core, 1.0, 0.0), 0.0)
        rows += dot(pick.astype(bf16), ref[...])
    rows = rows.astype(bf16)
    for first in range(0, FEATS, 768):
        out_ref[:, first : first + 768] = dot(rows, w_ref[:, first : first + 768]).astype(bf16)
    peaks = own_ref[...].astype(f32)
    peaks = peaks[:, 0:128] + peaks[:, 128:256] + peaks[:, 256:384]
    row = lax.broadcasted_iota(jnp.int32, peaks.shape, 0)
    mine = jnp.where(lax.rem(row, each) == EACH, lax.rem(row // each, RING), -1) == place[0]
    peak_ref[...] = jnp.max(jnp.where(mine, peaks, 0.0), axis=0, keepdims=True)


def out_terms(place, own, other, w_out):
    out = jax.ShapeDtypeStruct((ROWS, FEATS), bf16)
    return pl.pallas_call(
        out_kernel,
        grid_spec=pltpu.PrefetchScalarGridSpec(
            num_scalar_prefetch=1,
            grid=(1,),
            in_specs=[WHOLE] * 3,
            out_specs=[WHOLE] * 2,
        ),
        out_shape=[out, jax.ShapeDtypeStruct((1, 128), f32)],
        compiler_params=params(16),
        cost_estimate=cost(2 * ROWS * QCOLS * FEATS, 2 * (QCOLS * FEATS + ROWS * FEATS)),
    )(place, own, other, w_out)


def last_kernel(residual_ref, terms_ref, out_ref):
    total = residual_ref[...].astype(f32)
    for at in range(WIDE):
        total += terms_ref[at].astype(f32)
    out_ref[...] = total.astype(bf16)


def last(residual, terms):
    return pl.pallas_call(
        last_kernel,
        out_shape=jax.ShapeDtypeStruct(residual.shape, bf16),
        compiler_params=params(8),
        cost_estimate=cost(16 * residual.size, 36 * residual.size),
    )(residual, terms)


def scale_kernel(up_ref, peak_ref, out_ref):
    row = lax.broadcasted_iota(jnp.int32, (SHARE, 128), 0)
    lane = lax.broadcasted_iota(jnp.int32, (SHARE, 128), 1)
    column = jnp.sum(jnp.where(row == lane, peak_ref[...], 0.0), axis=1, keepdims=True)
    out_ref[...] = (up_ref[...] / (column + peak_eps)).astype(bf16)


def scale(up, peak):
    return pl.pallas_call(
        scale_kernel,
        out_shape=jax.ShapeDtypeStruct(up.shape, bf16),
        compiler_params=params(4),
        cost_estimate=cost(4 * up.size, 6 * up.size),
    )(up, peak)


def brought(shift, blocks):
    return [blocks[0]] + [shift(blocks[by], by) for by in range(1, RING)]


def added(shift, blocks):
    return sum((block.astype(f32) for block in brought(shift, blocks)[1:]), blocks[0].astype(f32))


def shards(residual, ln_gain, w_query, w_keyval, w_out, w_up, k_cache, v_cache, lengths):
    narrow, wide = lax.axis_index("narrow"), lax.axis_index("wide")
    place = jnp.stack([narrow >> 1, narrow & 1, wide >> 2, wide & 3]).astype(jnp.int32)
    residual_f32 = residual.astype(f32)
    sums = jnp.stack([jnp.sum(residual_f32, axis=1), jnp.sum(residual_f32 * residual_f32, axis=1)])
    sums = lax.all_to_all(jnp.broadcast_to(sums[None], (NARROW,) + sums.shape), "narrow", 0, 0, tiled=True)
    sums = jnp.sum(sums, axis=0)
    mean = sums[0] / D
    variance = sums[1] / D - mean * mean
    normed = (
        (residual_f32 - mean[:, None]) * lax.rsqrt(variance + norm_eps)[:, None] * ln_gain[None, :]
    ).astype(bf16)
    left, right = gathered(normed)

    keep, send, rows = head_terms(place, left, right, w_query, w_keyval)
    both = keep + swap_core(send)
    rows, both = lax.optimization_barrier((rows, both))
    query = added(shift_z, [both[by] for by in range(RING)]).astype(bf16)
    up_keep, up_send = up_terms(rows, w_up)
    query, up_keep, up_send = lax.optimization_barrier((query, up_keep, up_send))

    query = spread(query.reshape(WIDE, EACH, HCOLS)).reshape(WIDE, RING, EACH, HCOLS)
    query = query.transpose(1, 0, 2, 3).reshape(RING, SHARE, HCOLS)
    other = swap_core(query)
    keep = attend(False, place, lengths, query, k_cache, v_cache)
    send = attend(True, place, lengths, other, k_cache, v_cache)
    part, up, *blocks = pair(keep, swap_core(send), up_keep, swap_core(up_send))
    blocks = [shift_z(block, by + 1) for by, block in enumerate(blocks)]
    attended, up = finish(place, query, part, up, blocks)

    own = spread(attended.reshape(WIDE, EACH + 1, QCOLS)).reshape(WIDE * RING * (EACH + 1), QCOLS)
    terms, peak = out_terms(place, own, swap_core(own), w_out)
    terms = lax.all_to_all(terms.reshape(WIDE, LOCAL, FEATS), "wide", 0, 0, tiled=True)
    return (last(residual, terms), scale(up, peak), peak[0, :SHARE])


def solution(mesh):
    placed = (
        P("wide", "narrow"),
        P("narrow"),
        P("narrow", "wide"),
        P("narrow", "wide"),
        P("wide", "narrow"),
        P("narrow", "wide"),
        P("wide", "narrow", None),
        P("wide", "narrow", None),
        P("wide"),
    )
    return jax.shard_map(
        shards,
        mesh=mesh,
        in_specs=placed,
        out_specs=(P("wide", "narrow"), P("narrow", "wide"), P("narrow")),
        check_vma=False,
    )
```

```python
import functools

import jax
import jax.numpy as jnp
from jax import lax
from jax.experimental import pallas as pl
from jax.experimental.pallas import tpu as pltpu
from jax.sharding import PartitionSpec as P

D = 18432
HEADS = 48
HEAD = 256
WIDE = 16
NARROW = 8
RING = 4
ROWS = 384
LOCAL = ROWS // WIDE
EACH = LOCAL // NARROW
QCOLS = HEADS * HEAD // WIDE
HELD = QCOLS // HEAD
KVCOLS = 2 * HEAD // WIDE
HCOLS = QCOLS + 128
PACK = HEAD + 128
FEATS = D // NARROW
SHARE = ROWS // NARROW
UPCOLS = 36864 // WIDE
HALF = FEATS // 2
SPAN = RING * LOCAL

norm_eps = 1e-05
peak_eps = 1e-06

f32, bf16 = jnp.float32, jnp.bfloat16
SAME_CORE = [[w * NARROW + z * 2 + c for w in range(WIDE) for z in range(RING)] for c in range(2)]


def swap_core(x):
    return lax.ppermute(x, "narrow", [(i, i ^ 1) for i in range(NARROW)])


def shift_z(x, by):
    return lax.ppermute(x, "narrow", [(i, ((i // 2 + by) % RING) * 2 + i % 2) for i in range(NARROW)])


def shift_x(x, by):
    return lax.ppermute(x, "wide", [(i, ((i // RING + by) % RING) * RING + i % RING) for i in range(WIDE)])


def shift_y(x, by):
    return lax.ppermute(x, "wide", [(i, (i // RING) * RING + (i + by) % RING) for i in range(WIDE)])


def gathered(normed):
    left, right = normed[:, :HALF], normed[:, HALF:]
    left = jnp.concatenate([left] + [shift_x(left, by) for by in range(1, RING)])
    right = jnp.concatenate([right] + [shift_y(right, by) for by in range(1, RING)])
    return (
        [left] + [shift_y(left, by) for by in range(1, RING)],
        [right] + [shift_x(right, by) for by in range(1, RING)],
    )


def spread(x):
    x = jnp.broadcast_to(x[:, None], (WIDE, RING) + x.shape[1:]).reshape((WIDE * RING,) + x.shape[1:])
    return lax.all_to_all(x, ("wide", "narrow"), 0, 0, axis_index_groups=SAME_CORE, tiled=True)


def dot(a, b):
    return jnp.dot(a, b, preferred_element_type=f32)


def full(shape):
    return pl.BlockSpec(shape, lambda *_: (0,) * len(shape))


def params(mib):
    return pltpu.CompilerParams(vmem_limit_bytes=mib * 1024 * 1024)


def cost(flops, moved):
    return pl.CostEstimate(flops=int(flops), bytes_accessed=int(moved), transcendentals=0)


WHOLE = pl.BlockSpec(memory_space=pltpu.VMEM)


def slot_of(wide, z, c):
    to_z, to_c = lax.rem((wide >> 2) - z + RING, RING), (wide >> 1) & 1
    return ((to_c ^ c) * RING + to_z) * 2 + (wide & 1)


def held_in(slot, z, c):
    to_z, to_c = lax.rem((slot >> 1) % RING + z, RING), (slot >> 3) ^ c
    return (to_z * 2 + to_c) * 2 + (slot & 1)


def head_kernel(place, *refs):
    left, right = refs[:RING], refs[RING : 2 * RING]
    wq_ref, wkv_ref, keep_ref, send_ref, x_ref, acc_ref, rows_ref = refs[2 * RING :]
    z, c, x, y = place[0], place[1], place[2], place[3]
    for outer in range(RING):
        for first, ref in ((0, left[outer]), (HALF, right[outer])):
            held = ref[...].astype(f32)
            for inner in range(RING):
                by_x, by_y = (inner, outer) if first == 0 else (outer, inner)
                source = lax.rem(x - by_x + RING, RING) * RING + lax.rem(y - by_y + RING, RING)
                at = pl.ds(pl.multiple_of(slot_of(source, z, c) * LOCAL, 8), LOCAL)
                rows_ref[at, first : first + HALF] = held[inner * LOCAL : (inner + 1) * LOCAL]
    x_ref[...] = rows_ref[...].astype(bf16)

    def deal(terms, first):
        for at in range(WIDE):
            rows = pl.ds(pl.multiple_of(held_in(at, z, c) * LOCAL, 8), LOCAL)
            for lanes in range(terms.shape[1] // 128):
                acc_ref[lanes, rows, :] = terms[at * LOCAL : (at + 1) * LOCAL, lanes * 128 : (lanes + 1) * 128]
        for at in range(RING):
            n = lax.rem(z + at, RING) * 2
            for lanes in range(terms.shape[1] // 128):
                columns = slice(first + lanes * 128, first + (lanes + 1) * 128)
                keep_ref[at, :, columns] = acc_ref[lanes, pl.ds(n + c, SHARE, stride=NARROW), :]
                send_ref[at, :, columns] = acc_ref[lanes, pl.ds(n + 1 - c, SHARE, stride=NARROW), :]

    for first in range(0, QCOLS, 256):
        deal(dot(x_ref[...], wq_ref[:, first : first + 256]), first)
    deal(jnp.concatenate([dot(x_ref[...], wkv_ref[...]), jnp.zeros((ROWS, 128 - KVCOLS), f32)], axis=1), QCOLS)


def head_terms(place, left, right, w_query, w_keyval):
    out = jax.ShapeDtypeStruct((RING, SHARE, HCOLS), f32)
    rows = jax.ShapeDtypeStruct((ROWS, FEATS), bf16)
    return pl.pallas_call(
        head_kernel,
        grid_spec=pltpu.PrefetchScalarGridSpec(
            num_scalar_prefetch=1,
            grid=(1,),
            in_specs=[WHOLE] * (2 * RING + 2),
            out_specs=[WHOLE] * 3,
            scratch_shapes=[pltpu.VMEM((2, ROWS, 128), f32), pltpu.VMEM((ROWS, FEATS), f32)],
        ),
        out_shape=[out, out, rows],
        compiler_params=params(8),
        cost_estimate=cost(2 * ROWS * FEATS * (QCOLS + KVCOLS), 2 * FEATS * (ROWS + QCOLS + 128) + 8 * out.size),
    )(place, *left, *right, w_query, w_keyval)


def up_kernel(x_ref, w_ref, keep_ref, send_ref):
    half, tile = ROWS // 2, 768
    for first in range(0, UPCOLS, tile):
        columns = slice(first, first + tile)
        terms = dot(x_ref[...], w_ref[:, columns]).astype(bf16)
        for at in range(RING):
            keep_ref[at, :, columns] = terms[at * SHARE : (at + 1) * SHARE]
            send_ref[at, :, columns] = terms[half + at * SHARE : half + (at + 1) * SHARE]


def up_terms(x, w_up):
    out = jax.ShapeDtypeStruct((RING, SHARE, UPCOLS), bf16)
    return pl.pallas_call(
        up_kernel,
        in_specs=[WHOLE] * 2,
        out_specs=[WHOLE] * 2,
        out_shape=[out, out],
        compiler_params=params(4),
        cost_estimate=cost(2 * ROWS * FEATS * UPCOLS, 2 * (FEATS * (ROWS + UPCOLS) + ROWS * UPCOLS)),
    )(x, w_up)


def parts(value):
    high = value.astype(bf16).astype(f32)
    rest = value - high
    middle = rest.astype(bf16).astype(f32)
    return high, middle, (rest - middle).astype(bf16).astype(f32)


def packed(top, total):
    lane = lax.broadcasted_iota(jnp.int32, (top.shape[0], 128), 1)
    out = jnp.zeros(lane.shape, f32)
    for at, part in enumerate(parts(top) + parts(total)):
        out = jnp.where(lane == at, part, out)
    return out.astype(bf16)


def unpacked(block):
    held = block[:, HEAD:PACK].astype(f32)
    top = held[:, 0:1] + held[:, 1:2] + held[:, 2:3]
    total = held[:, 3:4] + held[:, 4:5] + held[:, 5:6]
    return block[:, :HEAD].astype(f32), top, total


def chosen(rows, columns, source):
    made = lax.broadcasted_iota(jnp.int32, (rows, columns), 0)
    held = lax.broadcasted_iota(jnp.int32, (rows, columns), 1)
    return jnp.where(source(made) == held, 1.0, 0.0).astype(bf16)


def by_row(block):
    return dot(chosen(SHARE, SHARE, lambda i: lax.rem(i, WIDE) * EACH + i // WIDE), block)


def heads_of(rows):
    return jnp.concatenate([rows[:, h * HEAD : (h + 1) * HEAD] for h in range(HELD)], axis=0)


def attend_kernel(away, place, lengths, q_ref, k_ref, v_ref, out_ref):
    positions = k_ref.shape[2]
    start = (place[0] * 2 + place[1]) * positions
    position = lax.broadcasted_iota(jnp.int32, (HEADS, positions), 1) + start
    for step in range(RING):
        group = group_of(away, step, place)
        rows = by_row(q_ref[lax.rem(place[0] + step, RING)])
        valid = jnp.concatenate([position < lengths[j * NARROW + group] for j in range(EACH)], axis=0)
        scores = jnp.concatenate(
            [
                lax.dot_general(
                    heads_of(rows[j * WIDE : (j + 1) * WIDE]).astype(bf16),
                    k_ref[j, group],
                    (((1,), (1,)), ((), ())),
                    preferred_element_type=f32,
                )
                for j in range(EACH)
            ],
            axis=0,
        )
        masked = jnp.where(valid, scores * (1.0 / HEAD**0.5), f32(-1e30))
        top = jnp.max(masked, axis=1, keepdims=True)
        probs = jnp.where(valid, jnp.exp(masked - top), f32(0.0))
        total = jnp.sum(probs, axis=1, keepdims=True)
        weights = probs.astype(bf16)
        for j in range(EACH):
            span = slice(j * HEADS, (j + 1) * HEADS)
            out_ref[step, span, :HEAD] = dot(weights[span], v_ref[j, group]).astype(bf16)
        out_ref[step, :, HEAD:] = packed(top, total)


def group_of(away, step, place):
    at = lax.rem(place[0] + step, RING) * 2
    return at + (1 - place[1] if away else place[1])


def attend(away, place, lengths, query, k_cache, v_cache):
    positions = k_cache.shape[1]
    k_cache = k_cache.reshape(EACH, NARROW, positions, HEAD)
    v_cache = v_cache.reshape(EACH, NARROW, positions, HEAD)
    out = jax.ShapeDtypeStruct((RING, EACH * HEADS, PACK), bf16)
    return pl.pallas_call(
        functools.partial(attend_kernel, away),
        grid_spec=pltpu.PrefetchScalarGridSpec(
            num_scalar_prefetch=2,
            grid=(1,),
            in_specs=[WHOLE] * 3,
            out_specs=WHOLE,
        ),
        out_shape=out,
        compiler_params=params(3),
        cost_estimate=cost(2 * LOCAL * HEADS * positions * HEAD, 2 * k_cache.size + 2 * out.size + 2 * query.size),
    )(place, lengths, query, k_cache, v_cache)


def joined(first, second):
    value_a, top_a, total_a = first
    value_b, top_b, total_b = second
    both = jnp.maximum(top_a, top_b)
    keep_a = jnp.exp(top_a - both)
    keep_b = jnp.exp(top_b - both)
    return value_a * keep_a + value_b * keep_b, both, total_a * keep_a + total_b * keep_b


def pair_kernel(a_ref, b_ref, up_a_ref, up_b_ref, own_ref, up_ref, *send_refs):
    for at in range(RING):
        value, top, total = joined(unpacked(a_ref[at]), unpacked(b_ref[at]))
        block = jnp.concatenate([value.astype(bf16), packed(top, total)], axis=1)
        up = up_a_ref[at].astype(f32) + up_b_ref[at].astype(f32)
        if at == 0:
            own_ref[...] = block
            up_ref[...] = up
        else:
            ref = send_refs[at - 1]
            for j in range(EACH):
                ref[:, j * PACK : (j + 1) * PACK] = block[j * HEADS : (j + 1) * HEADS]
            ref[:, EACH * PACK :] = up.astype(bf16)


def pair(a, b, up_a, up_b):
    out = [jax.ShapeDtypeStruct(a.shape[1:], bf16), jax.ShapeDtypeStruct(up_a.shape[1:], f32)]
    out += [jax.ShapeDtypeStruct((SHARE, EACH * PACK + UPCOLS), bf16)] * (RING - 1)
    return pl.pallas_call(
        pair_kernel,
        out_shape=out,
        compiler_params=params(3),
        cost_estimate=cost(4 * a.size, 6 * a.size + 6 * up_a.size),
    )(a, b, up_a, up_b)


def row_of(block):
    spot = lax.broadcasted_iota(jnp.int32, (KVCOLS, HEAD), 0)
    lane = lax.broadcasted_iota(jnp.int32, (KVCOLS, HEAD), 1)
    tiled = dot(block, (lax.rem(lane, KVCOLS) == spot).astype(bf16))
    row = lax.broadcasted_iota(jnp.int32, tiled.shape, 0)
    lane = lax.broadcasted_iota(jnp.int32, tiled.shape, 1)
    return jnp.sum(jnp.where(lane // KVCOLS == row, tiled, 0.0), axis=0, keepdims=True)


def finish_kernel(place, q_ref, own_ref, up_own_ref, *refs):
    blocks, (out_ref, up_ref) = refs[: RING - 1], refs[RING - 1 :]
    up = sum((ref[:, EACH * PACK :].astype(f32) for ref in blocks), up_own_ref[...])
    up_ref[...] = up
    rows = by_row(q_ref[place[0]])
    made = []
    for j in range(EACH):
        mine = rows[j * WIDE : (j + 1) * WIDE]
        query = heads_of(mine)
        keyval = mine[:, QCOLS : QCOLS + KVCOLS].astype(bf16)
        new_key = row_of(keyval[: WIDE // 2])
        new_value = row_of(keyval[WIDE // 2 :])
        own = jnp.sum(query * new_key, axis=1, keepdims=True) * (1.0 / HEAD**0.5)
        span = slice(j * HEADS, (j + 1) * HEADS)
        held = [own_ref[span, :]] + [ref[:, j * PACK : (j + 1) * PACK] for ref in blocks]
        value, top, total = functools.reduce(joined, [unpacked(block) for block in held])
        both = jnp.maximum(top, own)
        keep = jnp.exp(top - both)
        fresh = jnp.exp(own - both)
        mass = total * keep + fresh
        done = ((value * keep + fresh.astype(bf16).astype(f32) * new_value) / mass).astype(bf16)
        made.append(jnp.concatenate([done[h * WIDE : (h + 1) * WIDE] for h in range(HELD)], axis=1))
    each = EACH + 1
    order = chosen(WIDE * each, SHARE, lambda i: jnp.where(lax.rem(i, each) < EACH, lax.rem(i, each) * WIDE + i // each, -1))
    made = dot(order, jnp.concatenate(made, axis=0))
    column = jnp.max(jnp.abs(up), axis=1, keepdims=True)
    row = lax.broadcasted_iota(jnp.int32, (SHARE, 128), 0)
    lane = lax.broadcasted_iota(jnp.int32, (SHARE, 128), 1)
    peak = jnp.sum(jnp.where(row == lane, column, 0.0), axis=0, keepdims=True)
    peaks = jnp.concatenate(parts(peak) + (jnp.zeros((1, QCOLS - 3 * 128), f32),), axis=1)
    row = lax.broadcasted_iota(jnp.int32, made.shape, 0)
    out_ref[...] = jnp.where(lax.rem(row, each) == EACH, peaks, made).astype(bf16)


def finish(place, query, own, up_own, blocks):
    out = [
        jax.ShapeDtypeStruct((WIDE * (EACH + 1), QCOLS), bf16),
        jax.ShapeDtypeStruct(up_own.shape, f32),
    ]
    return pl.pallas_call(
        finish_kernel,
        grid_spec=pltpu.PrefetchScalarGridSpec(
            num_scalar_prefetch=1,
            grid=(1,),
            in_specs=[WHOLE] * (len(blocks) + 3),
            out_specs=[WHOLE] * 2,
        ),
        out_shape=out,
        compiler_params=params(3),
        cost_estimate=cost(40 * own.size, 10 * own.size + 14 * up_own.size),
    )(place, query, own, up_own, *blocks)


def out_kernel(place, own_ref, other_ref, w_ref, peak_ref, *out_refs):
    each = EACH + 1
    shape = (ROWS, own_ref.shape[0])
    made = lax.broadcasted_iota(jnp.int32, shape, 0)
    held = lax.broadcasted_iota(jnp.int32, shape, 1)
    at, local = made // LOCAL, lax.rem(made, LOCAL)
    group = lax.rem(local, NARROW)
    for along_x in (True, False):
        outer, inner = at // RING, lax.rem(at, RING)
        by_x, by_y = (outer, inner) if along_x else (inner, outer)
        wide = lax.rem(place[2] + by_x, RING) * RING + lax.rem(place[3] + by_y, RING)
        source = (wide * RING + group // 2) * each + local // NARROW
        rows = jnp.zeros((ROWS, QCOLS), f32)
        for core, ref in ((place[1], own_ref), (1 - place[1], other_ref)):
            pick = jnp.where(source == held, jnp.where(lax.rem(group, 2) == core, 1.0, 0.0), 0.0)
            rows += dot(pick.astype(bf16), ref[...])
        rows = rows.astype(bf16)
        refs = out_refs[:RING] if along_x else out_refs[RING:]
        start = 0 if along_x else HALF
        for first in range(0, HALF, 384):
            terms = dot(rows, w_ref[:, start + first : start + first + 384]).astype(bf16)
            for slot, ref in enumerate(refs):
                ref[:, first : first + 384] = terms[slot * SPAN : (slot + 1) * SPAN]
    peaks = own_ref[...].astype(f32)
    peaks = peaks[:, 0:128] + peaks[:, 128:256] + peaks[:, 256:384]
    row = lax.broadcasted_iota(jnp.int32, peaks.shape, 0)
    mine = jnp.where(lax.rem(row, each) == EACH, lax.rem(row // each, RING), -1) == place[0]
    peak_ref[...] = jnp.max(jnp.where(mine, peaks, 0.0), axis=0, keepdims=True)


def out_terms(place, own, other, w_out):
    return pl.pallas_call(
        out_kernel,
        grid_spec=pltpu.PrefetchScalarGridSpec(
            num_scalar_prefetch=1,
            grid=(1,),
            in_specs=[WHOLE] * 3,
            out_specs=[WHOLE] * (1 + 2 * RING),
        ),
        out_shape=[jax.ShapeDtypeStruct((1, 128), f32)] + [jax.ShapeDtypeStruct((SPAN, HALF), bf16)] * (2 * RING),
        compiler_params=params(6),
        cost_estimate=cost(2 * ROWS * QCOLS * FEATS, 2 * (QCOLS * FEATS + ROWS * FEATS)),
    )(place, own, other, w_out)


def middle_kernel(*refs):
    blocks, (own_ref, *send_refs) = refs[:RING], refs[RING:]
    total = sum((ref[...].astype(f32) for ref in blocks[1:]), blocks[0][...].astype(f32))
    own_ref[...] = total[:LOCAL]
    for at, ref in enumerate(send_refs):
        ref[...] = total[(at + 1) * LOCAL : (at + 2) * LOCAL].astype(bf16)


def middle(blocks):
    return pl.pallas_call(
        middle_kernel,
        out_shape=[jax.ShapeDtypeStruct((LOCAL, HALF), f32)] + [jax.ShapeDtypeStruct((LOCAL, HALF), bf16)] * (RING - 1),
        compiler_params=params(4),
        cost_estimate=cost(4 * blocks[0].size, 12 * blocks[0].size),
    )(*blocks)


def last_kernel(residual_ref, *refs):
    left, right, out_ref = refs[:RING], refs[RING : 2 * RING], refs[2 * RING]
    for first, blocks in ((0, left), (HALF, right)):
        total = sum((ref[...].astype(f32) for ref in blocks[1:]), blocks[0][...])
        columns = slice(first, first + HALF)
        out_ref[:, columns] = (residual_ref[:, columns].astype(f32) + total).astype(bf16)


def last(residual, left, right):
    return pl.pallas_call(
        last_kernel,
        out_shape=jax.ShapeDtypeStruct(residual.shape, bf16),
        compiler_params=params(2),
        cost_estimate=cost(8 * residual.size, 12 * residual.size),
    )(residual, *left, *right)


def scale_kernel(up_ref, peak_ref, out_ref):
    row = lax.broadcasted_iota(jnp.int32, (SHARE, 128), 0)
    lane = lax.broadcasted_iota(jnp.int32, (SHARE, 128), 1)
    column = jnp.sum(jnp.where(row == lane, peak_ref[...], 0.0), axis=1, keepdims=True)
    out_ref[...] = (up_ref[...] / (column + peak_eps)).astype(bf16)


def scale(up, peak):
    return pl.pallas_call(
        scale_kernel,
        out_shape=jax.ShapeDtypeStruct(up.shape, bf16),
        compiler_params=params(2),
        cost_estimate=cost(4 * up.size, 6 * up.size),
    )(up, peak)


def brought(shift, blocks):
    return [blocks[0]] + [shift(blocks[by], by) for by in range(1, RING)]


def added(shift, blocks):
    return sum((block.astype(f32) for block in brought(shift, blocks)[1:]), blocks[0].astype(f32))


def shards(residual, ln_gain, w_query, w_keyval, w_out, w_up, k_cache, v_cache, lengths):
    narrow, wide = lax.axis_index("narrow"), lax.axis_index("wide")
    place = jnp.stack([narrow >> 1, narrow & 1, wide >> 2, wide & 3]).astype(jnp.int32)
    residual_f32 = residual.astype(f32)
    sums = jnp.stack([jnp.sum(residual_f32, axis=1), jnp.sum(residual_f32 * residual_f32, axis=1)])
    sums = lax.all_to_all(jnp.broadcast_to(sums[None], (NARROW,) + sums.shape), "narrow", 0, 0, tiled=True)
    sums = jnp.sum(sums, axis=0)
    mean = sums[0] / D
    variance = sums[1] / D - mean * mean
    normed = (
        (residual_f32 - mean[:, None]) * lax.rsqrt(variance + norm_eps)[:, None] * ln_gain[None, :]
    ).astype(bf16)
    left, right = gathered(normed)

    keep, send, rows = head_terms(place, left, right, w_query, w_keyval)
    both = keep + swap_core(send)
    rows, both = lax.optimization_barrier((rows, both))
    query = added(shift_z, [both[by] for by in range(RING)]).astype(bf16)
    up_keep, up_send = up_terms(rows, w_up)
    query, up_keep, up_send = lax.optimization_barrier((query, up_keep, up_send))

    query = spread(query.reshape(WIDE, EACH, HCOLS)).reshape(WIDE, RING, EACH, HCOLS)
    query = query.transpose(1, 0, 2, 3).reshape(RING, SHARE, HCOLS)
    other = swap_core(query)
    keep = attend(False, place, lengths, query, k_cache, v_cache)
    send = attend(True, place, lengths, other, k_cache, v_cache)
    send, up_send = lax.optimization_barrier((send, up_send))
    part, up, *blocks = pair(keep, swap_core(send), up_keep, swap_core(up_send))
    blocks = [shift_z(block, by + 1) for by, block in enumerate(blocks)]
    attended, up = finish(place, query, part, up, blocks)

    own = spread(attended.reshape(WIDE, EACH + 1, QCOLS)).reshape(WIDE * RING * (EACH + 1), QCOLS)
    peak, *terms = out_terms(place, own, swap_core(own), w_out)
    left = middle(brought(shift_x, terms[:RING]))
    right = middle(brought(shift_y, terms[RING:]))
    mixed = last(residual, brought(shift_y, left), brought(shift_x, right))
    return (mixed, scale(up, peak), peak[0, :SHARE])


def solution(mesh):
    placed = (
        P("wide", "narrow"),
        P("narrow"),
        P("narrow", "wide"),
        P("narrow", "wide"),
        P("wide", "narrow"),
        P("narrow", "wide"),
        P("wide", "narrow", None),
        P("wide", "narrow", None),
        P("wide"),
    )
    return jax.shard_map(
        shards,
        mesh=mesh,
        in_specs=placed,
        out_specs=(P("wide", "narrow"), P("narrow", "wide"), P("narrow")),
        check_vma=False,
    )
```

```python
import functools

import jax
import jax.numpy as jnp
from jax import lax
from jax.experimental import pallas as pl
from jax.experimental.pallas import tpu as pltpu
from jax.sharding import PartitionSpec as P

D = 18432
HEADS = 48
HEAD = 256
WIDE = 16
NARROW = 8
RING = 4
ROWS = 384
LOCAL = ROWS // WIDE
EACH = LOCAL // NARROW
QCOLS = HEADS * HEAD // WIDE
HELD = QCOLS // HEAD
KVCOLS = 2 * HEAD // WIDE
HCOLS = QCOLS + 128
PACK = HEAD + 128
FEATS = D // NARROW
SHARE = ROWS // NARROW
UPCOLS = 36864 // WIDE
HALF = FEATS // 2
SPAN = RING * LOCAL
UP_PIECES = (256, 1024, 1024)

norm_eps = 1e-05
peak_eps = 1e-06

f32, bf16 = jnp.float32, jnp.bfloat16
SAME_CORE = [[w * NARROW + z * 2 + c for w in range(WIDE) for z in range(RING)] for c in range(2)]


def swap_core(x):
    return lax.ppermute(x, "narrow", [(i, i ^ 1) for i in range(NARROW)])


def shift_z(x, by):
    return lax.ppermute(x, "narrow", [(i, ((i // 2 + by) % RING) * 2 + i % 2) for i in range(NARROW)])


def shift_x(x, by):
    return lax.ppermute(x, "wide", [(i, ((i // RING + by) % RING) * RING + i % RING) for i in range(WIDE)])


def shift_y(x, by):
    return lax.ppermute(x, "wide", [(i, (i // RING) * RING + (i + by) % RING) for i in range(WIDE)])


def gathered(normed):
    left, right = normed[:, :HALF], normed[:, HALF:]
    left = jnp.concatenate([left] + [shift_x(left, by) for by in range(1, RING)])
    right = jnp.concatenate([right] + [shift_y(right, by) for by in range(1, RING)])
    return (
        [left] + [shift_y(left, by) for by in range(1, RING)],
        [right] + [shift_x(right, by) for by in range(1, RING)],
    )


def spread(x):
    x = jnp.broadcast_to(x[:, None], (WIDE, RING) + x.shape[1:]).reshape((WIDE * RING,) + x.shape[1:])
    return lax.all_to_all(x, ("wide", "narrow"), 0, 0, axis_index_groups=SAME_CORE, tiled=True)


def dot(a, b):
    return jnp.dot(a, b, preferred_element_type=f32)


def full(shape):
    return pl.BlockSpec(shape, lambda *_: (0,) * len(shape))


def params(mib):
    return pltpu.CompilerParams(vmem_limit_bytes=mib * 1024 * 1024)


def cost(flops, moved):
    return pl.CostEstimate(flops=int(flops), bytes_accessed=int(moved), transcendentals=0)


WHOLE = pl.BlockSpec(memory_space=pltpu.VMEM)
HBM = pl.BlockSpec(memory_space=pltpu.HBM)


def slot_of(wide, z, c):
    to_z, to_c = lax.rem((wide >> 2) - z + RING, RING), (wide >> 1) & 1
    return ((to_c ^ c) * RING + to_z) * 2 + (wide & 1)


def held_in(slot, z, c):
    to_z, to_c = lax.rem((slot >> 1) % RING + z, RING), (slot >> 3) ^ c
    return (to_z * 2 + to_c) * 2 + (slot & 1)


def head_kernel(place, *refs):
    left, right = refs[:RING], refs[RING : 2 * RING]
    wq_ref, wkv_ref, keep_ref, send_ref, x_ref, acc_ref, rows_ref = refs[2 * RING :]
    z, c, x, y = place[0], place[1], place[2], place[3]
    for outer in range(RING):
        for first, ref in ((0, left[outer]), (HALF, right[outer])):
            held = ref[...].astype(f32)
            for inner in range(RING):
                by_x, by_y = (inner, outer) if first == 0 else (outer, inner)
                source = lax.rem(x - by_x + RING, RING) * RING + lax.rem(y - by_y + RING, RING)
                at = pl.ds(pl.multiple_of(slot_of(source, z, c) * LOCAL, 8), LOCAL)
                rows_ref[at, first : first + HALF] = held[inner * LOCAL : (inner + 1) * LOCAL]
    x_ref[...] = rows_ref[...].astype(bf16)

    def deal(terms, first):
        for at in range(WIDE):
            rows = pl.ds(pl.multiple_of(held_in(at, z, c) * LOCAL, 8), LOCAL)
            for lanes in range(terms.shape[1] // 128):
                acc_ref[lanes, rows, :] = terms[at * LOCAL : (at + 1) * LOCAL, lanes * 128 : (lanes + 1) * 128]
        for at in range(RING):
            n = lax.rem(z + at, RING) * 2
            for lanes in range(terms.shape[1] // 128):
                columns = slice(first + lanes * 128, first + (lanes + 1) * 128)
                keep_ref[at, :, columns] = acc_ref[lanes, pl.ds(n + c, SHARE, stride=NARROW), :]
                send_ref[at, :, columns] = acc_ref[lanes, pl.ds(n + 1 - c, SHARE, stride=NARROW), :]

    for first in range(0, QCOLS, 256):
        deal(dot(x_ref[...], wq_ref[:, first : first + 256]), first)
    deal(jnp.concatenate([dot(x_ref[...], wkv_ref[...]), jnp.zeros((ROWS, 128 - KVCOLS), f32)], axis=1), QCOLS)


def head_terms(place, left, right, w_query, w_keyval):
    out = jax.ShapeDtypeStruct((RING, SHARE, HCOLS), f32)
    rows = jax.ShapeDtypeStruct((ROWS, FEATS), bf16)
    return pl.pallas_call(
        head_kernel,
        grid_spec=pltpu.PrefetchScalarGridSpec(
            num_scalar_prefetch=1,
            grid=(1,),
            in_specs=[WHOLE] * (2 * RING + 2),
            out_specs=[WHOLE] * 3,
            scratch_shapes=[pltpu.VMEM((2, ROWS, 128), f32), pltpu.VMEM((ROWS, FEATS), f32)],
        ),
        out_shape=[out, out, rows],
        compiler_params=params(8),
        cost_estimate=cost(2 * ROWS * FEATS * (QCOLS + KVCOLS), 2 * FEATS * (ROWS + QCOLS + 128) + 8 * out.size),
    )(place, *left, *right, w_query, w_keyval)


def up_kernel(x_ref, weights_ref, keep_ref, send_ref, w_ref, sum_ref, sem):
    half, tile = ROWS // 2, 768
    copies, spans, at = [], [], 0
    for count in UP_PIECES:
        span = slice(at, at + count)
        copies.append(pltpu.make_async_copy(weights_ref.at[span], w_ref.at[span], sem.at[len(spans)]))
        spans.append(span)
        at += count
    for copy in copies:
        copy.start()
    for piece, (copy, span) in enumerate(zip(copies, spans)):
        copy.wait()
        for first in range(0, UPCOLS, tile):
            columns = slice(first, first + tile)
            terms = dot(x_ref[:, span], w_ref[span, columns])
            if piece:
                terms += sum_ref[:, columns]
            if piece + 1 < len(spans):
                sum_ref[:, columns] = terms
                continue
            terms = terms.astype(bf16)
            for at in range(RING):
                keep_ref[at, :, columns] = terms[at * SHARE : (at + 1) * SHARE]
                send_ref[at, :, columns] = terms[half + at * SHARE : half + (at + 1) * SHARE]


def up_terms(x, w_up):
    out = jax.ShapeDtypeStruct((RING, SHARE, UPCOLS), bf16)
    return pl.pallas_call(
        up_kernel,
        in_specs=[WHOLE, HBM],
        out_specs=[WHOLE] * 2,
        out_shape=[out, out],
        scratch_shapes=[
            pltpu.VMEM(w_up.shape, bf16),
            pltpu.VMEM((ROWS, UPCOLS), f32),
            pltpu.SemaphoreType.DMA((len(UP_PIECES),)),
        ],
        compiler_params=params(48),
        cost_estimate=cost(2 * ROWS * FEATS * UPCOLS, 2 * (FEATS * (ROWS + UPCOLS) + ROWS * UPCOLS)),
    )(x, w_up)


def parts(value):
    high = value.astype(bf16).astype(f32)
    rest = value - high
    middle = rest.astype(bf16).astype(f32)
    return high, middle, (rest - middle).astype(bf16).astype(f32)


def packed(top, total):
    lane = lax.broadcasted_iota(jnp.int32, (top.shape[0], 128), 1)
    out = jnp.zeros(lane.shape, f32)
    for at, part in enumerate(parts(top) + parts(total)):
        out = jnp.where(lane == at, part, out)
    return out.astype(bf16)


def unpacked(block):
    held = block[:, HEAD:PACK].astype(f32)
    top = held[:, 0:1] + held[:, 1:2] + held[:, 2:3]
    total = held[:, 3:4] + held[:, 4:5] + held[:, 5:6]
    return block[:, :HEAD].astype(f32), top, total


def chosen(rows, columns, source):
    made = lax.broadcasted_iota(jnp.int32, (rows, columns), 0)
    held = lax.broadcasted_iota(jnp.int32, (rows, columns), 1)
    return jnp.where(source(made) == held, 1.0, 0.0).astype(bf16)


def by_row(block):
    return dot(chosen(SHARE, SHARE, lambda i: lax.rem(i, WIDE) * EACH + i // WIDE), block)


def heads_of(rows):
    return jnp.concatenate([rows[:, h * HEAD : (h + 1) * HEAD] for h in range(HELD)], axis=0)


def attend_kernel(away, place, lengths, q_ref, keys_ref, values_ref, out_ref, k_ref, v_ref, sem):
    groups = [group_of(away, step, place) for step in range(RING)]
    copies = [
        [pltpu.make_async_copy(source.at[:, group], held.at[step], sem.at[at, step]) for step, group in enumerate(groups)]
        for at, (source, held) in enumerate(((keys_ref, k_ref), (values_ref, v_ref)))
    ]
    for copy in copies[0] + copies[1]:
        copy.start()
    positions = k_ref.shape[2]
    start = (place[0] * 2 + place[1]) * positions
    position = lax.broadcasted_iota(jnp.int32, (HEADS, positions), 1) + start
    rows = [by_row(q_ref[lax.rem(place[0] + step, RING)]) for step in range(RING)]
    for copy in copies[0]:
        copy.wait()
    weights = []
    for step, group in enumerate(groups):
        valid = jnp.concatenate([position < lengths[j * NARROW + group] for j in range(EACH)], axis=0)
        scores = jnp.concatenate(
            [
                lax.dot_general(
                    heads_of(rows[step][j * WIDE : (j + 1) * WIDE]).astype(bf16),
                    k_ref[step, j],
                    (((1,), (1,)), ((), ())),
                    preferred_element_type=f32,
                )
                for j in range(EACH)
            ],
            axis=0,
        )
        masked = jnp.where(valid, scores * (1.0 / HEAD**0.5), f32(-1e30))
        top = jnp.max(masked, axis=1, keepdims=True)
        probs = jnp.where(valid, jnp.exp(masked - top), f32(0.0))
        out_ref[step, :, HEAD:] = packed(top, jnp.sum(probs, axis=1, keepdims=True))
        weights.append(probs.astype(bf16))
    for copy in copies[1]:
        copy.wait()
    for step in range(RING):
        for j in range(EACH):
            span = slice(j * HEADS, (j + 1) * HEADS)
            out_ref[step, span, :HEAD] = dot(weights[step][span], v_ref[step, j]).astype(bf16)


def group_of(away, step, place):
    at = lax.rem(place[0] + step, RING) * 2
    return at + (1 - place[1] if away else place[1])


def attend(away, place, lengths, query, k_cache, v_cache):
    positions = k_cache.shape[1]
    k_cache = k_cache.reshape(EACH, NARROW, positions, HEAD)
    v_cache = v_cache.reshape(EACH, NARROW, positions, HEAD)
    out = jax.ShapeDtypeStruct((RING, EACH * HEADS, PACK), bf16)
    return pl.pallas_call(
        functools.partial(attend_kernel, away),
        grid_spec=pltpu.PrefetchScalarGridSpec(
            num_scalar_prefetch=2,
            grid=(1,),
            in_specs=[WHOLE, HBM, HBM],
            out_specs=WHOLE,
            scratch_shapes=[pltpu.VMEM((RING, EACH, positions, HEAD), bf16)] * 2 + [pltpu.SemaphoreType.DMA((2, RING))],
        ),
        out_shape=out,
        compiler_params=params(53),
        cost_estimate=cost(2 * LOCAL * HEADS * positions * HEAD, 2 * k_cache.size + 2 * out.size + 2 * query.size),
    )(place, lengths, query, k_cache, v_cache)


def joined(first, second):
    value_a, top_a, total_a = first
    value_b, top_b, total_b = second
    both = jnp.maximum(top_a, top_b)
    keep_a = jnp.exp(top_a - both)
    keep_b = jnp.exp(top_b - both)
    return value_a * keep_a + value_b * keep_b, both, total_a * keep_a + total_b * keep_b


def pair_kernel(a_ref, b_ref, up_a_ref, up_b_ref, own_ref, up_ref, *send_refs):
    for at in range(RING):
        value, top, total = joined(unpacked(a_ref[at]), unpacked(b_ref[at]))
        block = jnp.concatenate([value.astype(bf16), packed(top, total)], axis=1)
        up = up_a_ref[at].astype(f32) + up_b_ref[at].astype(f32)
        if at == 0:
            own_ref[...] = block
            up_ref[...] = up
        else:
            ref = send_refs[at - 1]
            for j in range(EACH):
                ref[:, j * PACK : (j + 1) * PACK] = block[j * HEADS : (j + 1) * HEADS]
            ref[:, EACH * PACK :] = up.astype(bf16)


def pair(a, b, up_a, up_b):
    out = [jax.ShapeDtypeStruct(a.shape[1:], bf16), jax.ShapeDtypeStruct(up_a.shape[1:], f32)]
    out += [jax.ShapeDtypeStruct((SHARE, EACH * PACK + UPCOLS), bf16)] * (RING - 1)
    return pl.pallas_call(
        pair_kernel,
        out_shape=out,
        compiler_params=params(3),
        cost_estimate=cost(4 * a.size, 6 * a.size + 6 * up_a.size),
    )(a, b, up_a, up_b)


def row_of(block):
    spot = lax.broadcasted_iota(jnp.int32, (KVCOLS, HEAD), 0)
    lane = lax.broadcasted_iota(jnp.int32, (KVCOLS, HEAD), 1)
    tiled = dot(block, (lax.rem(lane, KVCOLS) == spot).astype(bf16))
    row = lax.broadcasted_iota(jnp.int32, tiled.shape, 0)
    lane = lax.broadcasted_iota(jnp.int32, tiled.shape, 1)
    return jnp.sum(jnp.where(lane // KVCOLS == row, tiled, 0.0), axis=0, keepdims=True)


def finish_kernel(place, q_ref, own_ref, up_own_ref, *refs):
    blocks, (out_ref, up_ref) = refs[: RING - 1], refs[RING - 1 :]
    up = sum((ref[:, EACH * PACK :].astype(f32) for ref in blocks), up_own_ref[...])
    up_ref[...] = up
    rows = by_row(q_ref[place[0]])
    made = []
    for j in range(EACH):
        mine = rows[j * WIDE : (j + 1) * WIDE]
        query = heads_of(mine)
        keyval = mine[:, QCOLS : QCOLS + KVCOLS].astype(bf16)
        new_key = row_of(keyval[: WIDE // 2])
        new_value = row_of(keyval[WIDE // 2 :])
        own = jnp.sum(query * new_key, axis=1, keepdims=True) * (1.0 / HEAD**0.5)
        span = slice(j * HEADS, (j + 1) * HEADS)
        held = [own_ref[span, :]] + [ref[:, j * PACK : (j + 1) * PACK] for ref in blocks]
        value, top, total = functools.reduce(joined, [unpacked(block) for block in held])
        both = jnp.maximum(top, own)
        keep = jnp.exp(top - both)
        fresh = jnp.exp(own - both)
        mass = total * keep + fresh
        done = ((value * keep + fresh.astype(bf16).astype(f32) * new_value) / mass).astype(bf16)
        made.append(jnp.concatenate([done[h * WIDE : (h + 1) * WIDE] for h in range(HELD)], axis=1))
    each = EACH + 1
    order = chosen(WIDE * each, SHARE, lambda i: jnp.where(lax.rem(i, each) < EACH, lax.rem(i, each) * WIDE + i // each, -1))
    made = dot(order, jnp.concatenate(made, axis=0))
    column = jnp.max(jnp.abs(up), axis=1, keepdims=True)
    row = lax.broadcasted_iota(jnp.int32, (SHARE, 128), 0)
    lane = lax.broadcasted_iota(jnp.int32, (SHARE, 128), 1)
    peak = jnp.sum(jnp.where(row == lane, column, 0.0), axis=0, keepdims=True)
    peaks = jnp.concatenate(parts(peak) + (jnp.zeros((1, QCOLS - 3 * 128), f32),), axis=1)
    row = lax.broadcasted_iota(jnp.int32, made.shape, 0)
    out_ref[...] = jnp.where(lax.rem(row, each) == EACH, peaks, made).astype(bf16)


def finish(place, query, own, up_own, blocks):
    out = [
        jax.ShapeDtypeStruct((WIDE * (EACH + 1), QCOLS), bf16),
        jax.ShapeDtypeStruct(up_own.shape, f32),
    ]
    return pl.pallas_call(
        finish_kernel,
        grid_spec=pltpu.PrefetchScalarGridSpec(
            num_scalar_prefetch=1,
            grid=(1,),
            in_specs=[WHOLE] * (len(blocks) + 3),
            out_specs=[WHOLE] * 2,
        ),
        out_shape=out,
        compiler_params=params(3),
        cost_estimate=cost(40 * own.size, 10 * own.size + 14 * up_own.size),
    )(place, query, own, up_own, *blocks)


def out_kernel(place, own_ref, other_ref, w_ref, peak_ref, *out_refs):
    each = EACH + 1
    shape = (ROWS, own_ref.shape[0])
    made = lax.broadcasted_iota(jnp.int32, shape, 0)
    held = lax.broadcasted_iota(jnp.int32, shape, 1)
    at, local = made // LOCAL, lax.rem(made, LOCAL)
    group = lax.rem(local, NARROW)
    for along_x in (True, False):
        outer, inner = at // RING, lax.rem(at, RING)
        by_x, by_y = (outer, inner) if along_x else (inner, outer)
        wide = lax.rem(place[2] + by_x, RING) * RING + lax.rem(place[3] + by_y, RING)
        source = (wide * RING + group // 2) * each + local // NARROW
        rows = jnp.zeros((ROWS, QCOLS), f32)
        for core, ref in ((place[1], own_ref), (1 - place[1], other_ref)):
            pick = jnp.where(source == held, jnp.where(lax.rem(group, 2) == core, 1.0, 0.0), 0.0)
            rows += dot(pick.astype(bf16), ref[...])
        rows = rows.astype(bf16)
        refs = out_refs[:RING] if along_x else out_refs[RING:]
        start = 0 if along_x else HALF
        for first in range(0, HALF, 384):
            terms = dot(rows, w_ref[:, start + first : start + first + 384]).astype(bf16)
            for slot, ref in enumerate(refs):
                ref[:, first : first + 384] = terms[slot * SPAN : (slot + 1) * SPAN]
    peaks = own_ref[...].astype(f32)
    peaks = peaks[:, 0:128] + peaks[:, 128:256] + peaks[:, 256:384]
    row = lax.broadcasted_iota(jnp.int32, peaks.shape, 0)
    mine = jnp.where(lax.rem(row, each) == EACH, lax.rem(row // each, RING), -1) == place[0]
    peak_ref[...] = jnp.max(jnp.where(mine, peaks, 0.0), axis=0, keepdims=True)


def out_terms(place, own, other, w_out):
    return pl.pallas_call(
        out_kernel,
        grid_spec=pltpu.PrefetchScalarGridSpec(
            num_scalar_prefetch=1,
            grid=(1,),
            in_specs=[WHOLE] * 3,
            out_specs=[WHOLE] * (1 + 2 * RING),
        ),
        out_shape=[jax.ShapeDtypeStruct((1, 128), f32)] + [jax.ShapeDtypeStruct((SPAN, HALF), bf16)] * (2 * RING),
        compiler_params=params(6),
        cost_estimate=cost(2 * ROWS * QCOLS * FEATS, 2 * (QCOLS * FEATS + ROWS * FEATS)),
    )(place, own, other, w_out)


def middle_kernel(*refs):
    blocks, (own_ref, *send_refs) = refs[:RING], refs[RING:]
    total = sum((ref[...].astype(f32) for ref in blocks[1:]), blocks[0][...].astype(f32))
    own_ref[...] = total[:LOCAL]
    for at, ref in enumerate(send_refs):
        ref[...] = total[(at + 1) * LOCAL : (at + 2) * LOCAL].astype(bf16)


def middle(blocks):
    return pl.pallas_call(
        middle_kernel,
        out_shape=[jax.ShapeDtypeStruct((LOCAL, HALF), f32)] + [jax.ShapeDtypeStruct((LOCAL, HALF), bf16)] * (RING - 1),
        compiler_params=params(4),
        cost_estimate=cost(4 * blocks[0].size, 12 * blocks[0].size),
    )(*blocks)


def last_kernel(residual_ref, *refs):
    left, right, out_ref = refs[:RING], refs[RING : 2 * RING], refs[2 * RING]
    for first, blocks in ((0, left), (HALF, right)):
        total = sum((ref[...].astype(f32) for ref in blocks[1:]), blocks[0][...])
        columns = slice(first, first + HALF)
        out_ref[:, columns] = (residual_ref[:, columns].astype(f32) + total).astype(bf16)


def last(residual, left, right):
    return pl.pallas_call(
        last_kernel,
        out_shape=jax.ShapeDtypeStruct(residual.shape, bf16),
        compiler_params=params(2),
        cost_estimate=cost(8 * residual.size, 12 * residual.size),
    )(residual, *left, *right)


def scale_kernel(up_ref, peak_ref, out_ref):
    row = lax.broadcasted_iota(jnp.int32, (SHARE, 128), 0)
    lane = lax.broadcasted_iota(jnp.int32, (SHARE, 128), 1)
    column = jnp.sum(jnp.where(row == lane, peak_ref[...], 0.0), axis=1, keepdims=True)
    out_ref[...] = (up_ref[...] / (column + peak_eps)).astype(bf16)


def scale(up, peak):
    return pl.pallas_call(
        scale_kernel,
        out_shape=jax.ShapeDtypeStruct(up.shape, bf16),
        compiler_params=params(2),
        cost_estimate=cost(4 * up.size, 6 * up.size),
    )(up, peak)


def brought(shift, blocks):
    return [blocks[0]] + [shift(blocks[by], by) for by in range(1, RING)]


def added(shift, blocks):
    return sum((block.astype(f32) for block in brought(shift, blocks)[1:]), blocks[0].astype(f32))


def shards(residual, ln_gain, w_query, w_keyval, w_out, w_up, k_cache, v_cache, lengths):
    narrow, wide = lax.axis_index("narrow"), lax.axis_index("wide")
    place = jnp.stack([narrow >> 1, narrow & 1, wide >> 2, wide & 3]).astype(jnp.int32)
    residual_f32 = residual.astype(f32)
    sums = jnp.stack([jnp.sum(residual_f32, axis=1), jnp.sum(residual_f32 * residual_f32, axis=1)])
    sums = lax.all_to_all(jnp.broadcast_to(sums[None], (NARROW,) + sums.shape), "narrow", 0, 0, tiled=True)
    sums = jnp.sum(sums, axis=0)
    mean = sums[0] / D
    variance = sums[1] / D - mean * mean
    normed = (
        (residual_f32 - mean[:, None]) * lax.rsqrt(variance + norm_eps)[:, None] * ln_gain[None, :]
    ).astype(bf16)
    left, right = gathered(normed)

    keep, send, rows = head_terms(place, left, right, w_query, w_keyval)
    both = keep + swap_core(send)
    rows, both = lax.optimization_barrier((rows, both))
    query = added(shift_z, [both[by] for by in range(RING)]).astype(bf16)
    up_keep, up_send = up_terms(rows, w_up)
    query, up_keep, up_send = lax.optimization_barrier((query, up_keep, up_send))

    query = spread(query.reshape(WIDE, EACH, HCOLS)).reshape(WIDE, RING, EACH, HCOLS)
    query = query.transpose(1, 0, 2, 3).reshape(RING, SHARE, HCOLS)
    other = swap_core(query)
    keep = attend(False, place, lengths, query, k_cache, v_cache)
    send = attend(True, place, lengths, other, k_cache, v_cache)
    send, up_send = lax.optimization_barrier((send, up_send))
    part, up, *blocks = pair(keep, swap_core(send), up_keep, swap_core(up_send))
    blocks = [shift_z(block, by + 1) for by, block in enumerate(blocks)]
    attended, up = finish(place, query, part, up, blocks)

    own = spread(attended.reshape(WIDE, EACH + 1, QCOLS)).reshape(WIDE * RING * (EACH + 1), QCOLS)
    peak, *terms = out_terms(place, own, swap_core(own), w_out)
    left = middle(brought(shift_x, terms[:RING]))
    right = middle(brought(shift_y, terms[RING:]))
    mixed = last(residual, brought(shift_y, left), brought(shift_x, right))
    return (mixed, scale(up, peak), peak[0, :SHARE])


def solution(mesh):
    placed = (
        P("wide", "narrow"),
        P("narrow"),
        P("narrow", "wide"),
        P("narrow", "wide"),
        P("wide", "narrow"),
        P("narrow", "wide"),
        P("wide", "narrow", None),
        P("wide", "narrow", None),
        P("wide"),
    )
    return jax.shard_map(
        shards,
        mesh=mesh,
        in_specs=placed,
        out_specs=(P("wide", "narrow"), P("narrow", "wide"), P("narrow")),
        check_vma=False,
    )
```

```python
import functools

import jax
import jax.numpy as jnp
from jax import lax
from jax.experimental import pallas as pl
from jax.experimental.pallas import tpu as pltpu
from jax.sharding import PartitionSpec as P

D = 18432
HEADS = 48
HEAD = 256
WIDE = 16
NARROW = 8
RING = 4
ROWS = 384
LOCAL = ROWS // WIDE
EACH = LOCAL // NARROW
QCOLS = HEADS * HEAD // WIDE
HELD = QCOLS // HEAD
KVCOLS = 2 * HEAD // WIDE
HCOLS = QCOLS + 128
PACK = EACH * HEAD + 128
FEATS = D // NARROW
SHARE = ROWS // NARROW
UPCOLS = 36864 // WIDE
GATHERED = 1280
SUMMED = 1152
SPAN = RING * LOCAL
UP_PIECES = (256, 1024, 1024)

norm_eps = 1e-05
peak_eps = 1e-06

f32, bf16 = jnp.float32, jnp.bfloat16
SAME_CORE = [[w * NARROW + z * 2 + c for w in range(WIDE) for z in range(RING)] for c in range(2)]


def swap_core(x):
    return lax.ppermute(x, "narrow", [(i, i ^ 1) for i in range(NARROW)])


def shift_z(x, by):
    return lax.ppermute(x, "narrow", [(i, ((i // 2 + by) % RING) * 2 + i % 2) for i in range(NARROW)])


def shift_x(x, by):
    return lax.ppermute(x, "wide", [(i, ((i // RING + by) % RING) * RING + i % RING) for i in range(WIDE)])


def shift_y(x, by):
    return lax.ppermute(x, "wide", [(i, (i // RING) * RING + (i + by) % RING) for i in range(WIDE)])


def gathered(normed):
    left, right = normed[:, :GATHERED], normed[:, GATHERED:]
    left = jnp.concatenate([left] + [shift_x(left, by) for by in range(1, RING)])
    right = jnp.concatenate([right] + [shift_y(right, by) for by in range(1, RING)])
    return (
        [left] + [shift_y(left, by) for by in range(1, RING)],
        [right] + [shift_x(right, by) for by in range(1, RING)],
    )


def spread(x):
    x = jnp.broadcast_to(x[:, None], (WIDE, RING) + x.shape[1:]).reshape((WIDE * RING,) + x.shape[1:])
    return lax.all_to_all(x, ("wide", "narrow"), 0, 0, axis_index_groups=SAME_CORE, tiled=True)


def dot(a, b):
    return jnp.dot(a, b, preferred_element_type=f32)


def full(shape):
    return pl.BlockSpec(shape, lambda *_: (0,) * len(shape))


def params(mib):
    return pltpu.CompilerParams(vmem_limit_bytes=mib * 1024 * 1024)


def cost(flops, moved):
    return pl.CostEstimate(flops=int(flops), bytes_accessed=int(moved), transcendentals=0)


WHOLE = pl.BlockSpec(memory_space=pltpu.VMEM)
HBM = pl.BlockSpec(memory_space=pltpu.HBM)


def slot_of(wide, z, c):
    to_z, to_c = lax.rem((wide >> 2) - z + RING, RING), (wide >> 1) & 1
    return ((to_c ^ c) * RING + to_z) * 2 + (wide & 1)


def held_in(slot, z, c):
    to_z, to_c = lax.rem((slot >> 1) % RING + z, RING), (slot >> 3) ^ c
    return (to_z * 2 + to_c) * 2 + (slot & 1)


def head_kernel(place, *refs):
    left, right = refs[:RING], refs[RING : 2 * RING]
    wq_ref, wkv_ref, keep_ref, send_ref, x_ref, acc_ref, rows_ref = refs[2 * RING :]
    z, c, x, y = place[0], place[1], place[2], place[3]
    for outer in range(RING):
        for first, ref in ((0, left[outer]), (GATHERED, right[outer])):
            held = ref[...].astype(f32)
            for inner in range(RING):
                by_x, by_y = (inner, outer) if first == 0 else (outer, inner)
                source = lax.rem(x - by_x + RING, RING) * RING + lax.rem(y - by_y + RING, RING)
                at = pl.ds(pl.multiple_of(slot_of(source, z, c) * LOCAL, 8), LOCAL)
                rows_ref[at, first : first + held.shape[1]] = held[inner * LOCAL : (inner + 1) * LOCAL]
    x_ref[...] = rows_ref[...].astype(bf16)

    def deal(terms, first):
        for at in range(WIDE):
            rows = pl.ds(pl.multiple_of(held_in(at, z, c) * LOCAL, 8), LOCAL)
            for lanes in range(terms.shape[1] // 128):
                acc_ref[lanes, rows, :] = terms[at * LOCAL : (at + 1) * LOCAL, lanes * 128 : (lanes + 1) * 128]
        for at in range(RING):
            n = lax.rem(z + at, RING) * 2
            for lanes in range(terms.shape[1] // 128):
                columns = slice(first + lanes * 128, first + (lanes + 1) * 128)
                keep_ref[at, :, columns] = acc_ref[lanes, pl.ds(n + c, SHARE, stride=NARROW), :]
                send_ref[at, :, columns] = acc_ref[lanes, pl.ds(n + 1 - c, SHARE, stride=NARROW), :]

    for first in range(0, QCOLS, 256):
        deal(dot(x_ref[...], wq_ref[:, first : first + 256]), first)
    deal(jnp.concatenate([dot(x_ref[...], wkv_ref[...]), jnp.zeros((ROWS, 128 - KVCOLS), f32)], axis=1), QCOLS)


def head_terms(place, left, right, w_query, w_keyval):
    out = jax.ShapeDtypeStruct((RING, SHARE, HCOLS), f32)
    rows = jax.ShapeDtypeStruct((ROWS, FEATS), bf16)
    return pl.pallas_call(
        head_kernel,
        grid_spec=pltpu.PrefetchScalarGridSpec(
            num_scalar_prefetch=1,
            grid=(1,),
            in_specs=[WHOLE] * (2 * RING + 2),
            out_specs=[WHOLE] * 3,
            scratch_shapes=[pltpu.VMEM((2, ROWS, 128), f32), pltpu.VMEM((ROWS, FEATS), f32)],
        ),
        out_shape=[out, out, rows],
        compiler_params=params(8),
        cost_estimate=cost(2 * ROWS * FEATS * (QCOLS + KVCOLS), 2 * FEATS * (ROWS + QCOLS + 128) + 8 * out.size),
    )(place, *left, *right, w_query, w_keyval)


def up_kernel(x_ref, weights_ref, keep_ref, send_ref, w_ref, sum_ref, sem):
    half, tile = ROWS // 2, 768
    copies, spans, at = [], [], 0
    for count in UP_PIECES:
        span = slice(at, at + count)
        copies.append(pltpu.make_async_copy(weights_ref.at[span], w_ref.at[span], sem.at[len(spans)]))
        spans.append(span)
        at += count
    for copy in copies:
        copy.start()
    for piece, (copy, span) in enumerate(zip(copies, spans)):
        copy.wait()
        for first in range(0, UPCOLS, tile):
            columns = slice(first, first + tile)
            terms = dot(x_ref[:, span], w_ref[span, columns])
            if piece:
                terms += sum_ref[:, columns]
            if piece + 1 < len(spans):
                sum_ref[:, columns] = terms
                continue
            terms = terms.astype(bf16)
            for at in range(RING):
                keep_ref[at, :, columns] = terms[at * SHARE : (at + 1) * SHARE]
                send_ref[at, :, columns] = terms[half + at * SHARE : half + (at + 1) * SHARE]


def up_terms(x, w_up):
    out = jax.ShapeDtypeStruct((RING, SHARE, UPCOLS), bf16)
    return pl.pallas_call(
        up_kernel,
        in_specs=[WHOLE, HBM],
        out_specs=[WHOLE] * 2,
        out_shape=[out, out],
        scratch_shapes=[
            pltpu.VMEM(w_up.shape, bf16),
            pltpu.VMEM((ROWS, UPCOLS), f32),
            pltpu.SemaphoreType.DMA((len(UP_PIECES),)),
        ],
        compiler_params=params(48),
        cost_estimate=cost(2 * ROWS * FEATS * UPCOLS, 2 * (FEATS * (ROWS + UPCOLS) + ROWS * UPCOLS)),
    )(x, w_up)


def parts(value):
    high = value.astype(bf16).astype(f32)
    rest = value - high
    middle = rest.astype(bf16).astype(f32)
    return high, middle, (rest - middle).astype(bf16).astype(f32)


def packed(tops, totals):
    lane = lax.broadcasted_iota(jnp.int32, (tops[0].shape[0], 128), 1)
    out = jnp.zeros(lane.shape, f32)
    for j, (top, total) in enumerate(zip(tops, totals)):
        for at, part in enumerate(parts(top) + parts(total)):
            out = jnp.where(lane == 6 * j + at, part, out)
    return out.astype(bf16)


def unpacked(block, j):
    held = block[:, EACH * HEAD : PACK].astype(f32)
    lanes = [held[:, 6 * j + at : 6 * j + at + 1] for at in range(6)]
    return block[:, j * HEAD : (j + 1) * HEAD].astype(f32), lanes[0] + lanes[1] + lanes[2], lanes[3] + lanes[4] + lanes[5]


def chosen(rows, columns, source):
    made = lax.broadcasted_iota(jnp.int32, (rows, columns), 0)
    held = lax.broadcasted_iota(jnp.int32, (rows, columns), 1)
    return jnp.where(source(made) == held, 1.0, 0.0).astype(bf16)


def by_row(block):
    return dot(chosen(SHARE, SHARE, lambda i: lax.rem(i, WIDE) * EACH + i // WIDE), block)


def heads_of(rows):
    return jnp.concatenate([rows[:, h * HEAD : (h + 1) * HEAD] for h in range(HELD)], axis=0)


def attend_kernel(away, place, lengths, q_ref, keys_ref, values_ref, out_ref, k_ref, v_ref, sem):
    groups = [group_of(away, step, place) for step in range(RING)]
    copies = [
        [pltpu.make_async_copy(source.at[:, group], held.at[step], sem.at[at, step]) for step, group in enumerate(groups)]
        for at, (source, held) in enumerate(((keys_ref, k_ref), (values_ref, v_ref)))
    ]
    for copy in copies[0] + copies[1]:
        copy.start()
    positions = k_ref.shape[2]
    start = (place[0] * 2 + place[1]) * positions
    position = lax.broadcasted_iota(jnp.int32, (HEADS, positions), 1) + start
    rows = [by_row(q_ref[lax.rem(place[0] + step, RING)]) for step in range(RING)]
    for copy in copies[0]:
        copy.wait()
    weights = []
    for step, group in enumerate(groups):
        valid = jnp.concatenate([position < lengths[j * NARROW + group] for j in range(EACH)], axis=0)
        scores = jnp.concatenate(
            [
                lax.dot_general(
                    heads_of(rows[step][j * WIDE : (j + 1) * WIDE]).astype(bf16),
                    k_ref[step, j],
                    (((1,), (1,)), ((), ())),
                    preferred_element_type=f32,
                )
                for j in range(EACH)
            ],
            axis=0,
        )
        masked = jnp.where(valid, scores * (1.0 / HEAD**0.5), f32(-1e30))
        top = jnp.max(masked, axis=1, keepdims=True)
        probs = jnp.where(valid, jnp.exp(masked - top), f32(0.0))
        total = jnp.sum(probs, axis=1, keepdims=True)
        spans = [slice(j * HEADS, (j + 1) * HEADS) for j in range(EACH)]
        out_ref[step, :, EACH * HEAD :] = packed([top[span] for span in spans], [total[span] for span in spans])
        weights.append(probs.astype(bf16))
    for copy in copies[1]:
        copy.wait()
    for step in range(RING):
        for j in range(EACH):
            span = slice(j * HEADS, (j + 1) * HEADS)
            out_ref[step, :, j * HEAD : (j + 1) * HEAD] = dot(weights[step][span], v_ref[step, j]).astype(bf16)


def group_of(away, step, place):
    at = lax.rem(place[0] + step, RING) * 2
    return at + (1 - place[1] if away else place[1])


def attend(away, place, lengths, query, k_cache, v_cache):
    positions = k_cache.shape[1]
    k_cache = k_cache.reshape(EACH, NARROW, positions, HEAD)
    v_cache = v_cache.reshape(EACH, NARROW, positions, HEAD)
    out = jax.ShapeDtypeStruct((RING, HEADS, PACK), bf16)
    return pl.pallas_call(
        functools.partial(attend_kernel, away),
        grid_spec=pltpu.PrefetchScalarGridSpec(
            num_scalar_prefetch=2,
            grid=(1,),
            in_specs=[WHOLE, HBM, HBM],
            out_specs=WHOLE,
            scratch_shapes=[pltpu.VMEM((RING, EACH, positions, HEAD), bf16)] * 2 + [pltpu.SemaphoreType.DMA((2, RING))],
        ),
        out_shape=out,
        compiler_params=params(53),
        cost_estimate=cost(2 * LOCAL * HEADS * positions * HEAD, 2 * k_cache.size + 2 * out.size + 2 * query.size),
    )(place, lengths, query, k_cache, v_cache)


def joined(first, second):
    value_a, top_a, total_a = first
    value_b, top_b, total_b = second
    both = jnp.maximum(top_a, top_b)
    keep_a = jnp.exp(top_a - both)
    keep_b = jnp.exp(top_b - both)
    return value_a * keep_a + value_b * keep_b, both, total_a * keep_a + total_b * keep_b


def pair_kernel(a_ref, b_ref, up_a_ref, up_b_ref, own_ref, up_ref, *send_refs):
    for at in range(RING):
        made = [joined(unpacked(a_ref[at], j), unpacked(b_ref[at], j)) for j in range(EACH)]
        block = jnp.concatenate(
            [value.astype(bf16) for value, _, _ in made] + [packed([top for _, top, _ in made], [total for _, _, total in made])],
            axis=1,
        )
        up = up_a_ref[at].astype(f32) + up_b_ref[at].astype(f32)
        if at == 0:
            own_ref[...] = block
            up_ref[...] = up
        else:
            ref = send_refs[at - 1]
            ref[:, :PACK] = block
            ref[:, PACK:] = up.astype(bf16)


def pair(a, b, up_a, up_b):
    out = [jax.ShapeDtypeStruct(a.shape[1:], bf16), jax.ShapeDtypeStruct(up_a.shape[1:], f32)]
    out += [jax.ShapeDtypeStruct((SHARE, PACK + UPCOLS), bf16)] * (RING - 1)
    return pl.pallas_call(
        pair_kernel,
        out_shape=out,
        compiler_params=params(3),
        cost_estimate=cost(4 * a.size, 6 * a.size + 6 * up_a.size),
    )(a, b, up_a, up_b)


def row_of(block):
    spot = lax.broadcasted_iota(jnp.int32, (KVCOLS, HEAD), 0)
    lane = lax.broadcasted_iota(jnp.int32, (KVCOLS, HEAD), 1)
    tiled = dot(block, (lax.rem(lane, KVCOLS) == spot).astype(bf16))
    row = lax.broadcasted_iota(jnp.int32, tiled.shape, 0)
    lane = lax.broadcasted_iota(jnp.int32, tiled.shape, 1)
    return jnp.sum(jnp.where(lane // KVCOLS == row, tiled, 0.0), axis=0, keepdims=True)


def finish_kernel(place, q_ref, own_ref, up_own_ref, *refs):
    blocks, (out_ref, up_ref) = refs[: RING - 1], refs[RING - 1 :]
    up = sum((ref[:, PACK:].astype(f32) for ref in blocks), up_own_ref[...])
    up_ref[...] = up
    rows = by_row(q_ref[place[0]])
    made = []
    for j in range(EACH):
        mine = rows[j * WIDE : (j + 1) * WIDE]
        query = heads_of(mine)
        keyval = mine[:, QCOLS : QCOLS + KVCOLS].astype(bf16)
        new_key = row_of(keyval[: WIDE // 2])
        new_value = row_of(keyval[WIDE // 2 :])
        own = jnp.sum(query * new_key, axis=1, keepdims=True) * (1.0 / HEAD**0.5)
        value, top, total = functools.reduce(joined, [unpacked(ref, j) for ref in (own_ref, *blocks)])
        both = jnp.maximum(top, own)
        keep = jnp.exp(top - both)
        fresh = jnp.exp(own - both)
        mass = total * keep + fresh
        done = ((value * keep + fresh.astype(bf16).astype(f32) * new_value) / mass).astype(bf16)
        made.append(jnp.concatenate([done[h * WIDE : (h + 1) * WIDE] for h in range(HELD)], axis=1))
    each = EACH + 1
    order = chosen(WIDE * each, SHARE, lambda i: jnp.where(lax.rem(i, each) < EACH, lax.rem(i, each) * WIDE + i // each, -1))
    made = dot(order, jnp.concatenate(made, axis=0))
    column = jnp.max(jnp.abs(up), axis=1, keepdims=True)
    row = lax.broadcasted_iota(jnp.int32, (SHARE, 128), 0)
    lane = lax.broadcasted_iota(jnp.int32, (SHARE, 128), 1)
    peak = jnp.sum(jnp.where(row == lane, column, 0.0), axis=0, keepdims=True)
    peaks = jnp.concatenate(parts(peak) + (jnp.zeros((1, QCOLS - 3 * 128), f32),), axis=1)
    row = lax.broadcasted_iota(jnp.int32, made.shape, 0)
    out_ref[...] = jnp.where(lax.rem(row, each) == EACH, peaks, made).astype(bf16)


def finish(place, query, own, up_own, blocks):
    out = [
        jax.ShapeDtypeStruct((WIDE * (EACH + 1), QCOLS), bf16),
        jax.ShapeDtypeStruct(up_own.shape, f32),
    ]
    return pl.pallas_call(
        finish_kernel,
        grid_spec=pltpu.PrefetchScalarGridSpec(
            num_scalar_prefetch=1,
            grid=(1,),
            in_specs=[WHOLE] * (len(blocks) + 3),
            out_specs=[WHOLE] * 2,
        ),
        out_shape=out,
        compiler_params=params(3),
        cost_estimate=cost(40 * own.size, 10 * own.size + 14 * up_own.size),
    )(place, query, own, up_own, *blocks)


def out_kernel(place, own_ref, other_ref, w_ref, peak_ref, *out_refs):
    each = EACH + 1
    shape = (ROWS, own_ref.shape[0])
    made = lax.broadcasted_iota(jnp.int32, shape, 0)
    held = lax.broadcasted_iota(jnp.int32, shape, 1)
    at, local = made // LOCAL, lax.rem(made, LOCAL)
    group = lax.rem(local, NARROW)
    for along_x in (True, False):
        outer, inner = at // RING, lax.rem(at, RING)
        by_x, by_y = (outer, inner) if along_x else (inner, outer)
        wide = lax.rem(place[2] + by_x, RING) * RING + lax.rem(place[3] + by_y, RING)
        source = (wide * RING + group // 2) * each + local // NARROW
        rows = jnp.zeros((ROWS, QCOLS), f32)
        for core, ref in ((place[1], own_ref), (1 - place[1], other_ref)):
            pick = jnp.where(source == held, jnp.where(lax.rem(group, 2) == core, 1.0, 0.0), 0.0)
            rows += dot(pick.astype(bf16), ref[...])
        rows = rows.astype(bf16)
        refs = out_refs[:RING] if along_x else out_refs[RING:]
        start, width = (0, SUMMED) if along_x else (SUMMED, FEATS - SUMMED)
        for first in range(0, width, 384):
            terms = dot(rows, w_ref[:, start + first : start + first + 384]).astype(bf16)
            for slot, ref in enumerate(refs):
                ref[:, first : first + 384] = terms[slot * SPAN : (slot + 1) * SPAN]
    peaks = own_ref[...].astype(f32)
    peaks = peaks[:, 0:128] + peaks[:, 128:256] + peaks[:, 256:384]
    row = lax.broadcasted_iota(jnp.int32, peaks.shape, 0)
    mine = jnp.where(lax.rem(row, each) == EACH, lax.rem(row // each, RING), -1) == place[0]
    peak_ref[...] = jnp.max(jnp.where(mine, peaks, 0.0), axis=0, keepdims=True)


def out_terms(place, own, other, w_out):
    return pl.pallas_call(
        out_kernel,
        grid_spec=pltpu.PrefetchScalarGridSpec(
            num_scalar_prefetch=1,
            grid=(1,),
            in_specs=[WHOLE] * 3,
            out_specs=[WHOLE] * (1 + 2 * RING),
        ),
        out_shape=[jax.ShapeDtypeStruct((1, 128), f32)]
        + [jax.ShapeDtypeStruct((SPAN, SUMMED), bf16)] * RING
        + [jax.ShapeDtypeStruct((SPAN, FEATS - SUMMED), bf16)] * RING,
        compiler_params=params(6),
        cost_estimate=cost(2 * ROWS * QCOLS * FEATS, 2 * (QCOLS * FEATS + ROWS * FEATS)),
    )(place, own, other, w_out)


def middle_kernel(*refs):
    blocks, (own_ref, *send_refs) = refs[:RING], refs[RING:]
    total = sum((ref[...].astype(f32) for ref in blocks[1:]), blocks[0][...].astype(f32))
    own_ref[...] = total[:LOCAL]
    for at, ref in enumerate(send_refs):
        ref[...] = total[(at + 1) * LOCAL : (at + 2) * LOCAL].astype(bf16)


def middle(blocks):
    width = blocks[0].shape[1]
    return pl.pallas_call(
        middle_kernel,
        out_shape=[jax.ShapeDtypeStruct((LOCAL, width), f32)] + [jax.ShapeDtypeStruct((LOCAL, width), bf16)] * (RING - 1),
        compiler_params=params(4),
        cost_estimate=cost(4 * blocks[0].size, 12 * blocks[0].size),
    )(*blocks)


def last_kernel(residual_ref, *refs):
    left, right, out_ref = refs[:RING], refs[RING : 2 * RING], refs[2 * RING]
    for first, blocks in ((0, left), (SUMMED, right)):
        total = sum((ref[...].astype(f32) for ref in blocks[1:]), blocks[0][...])
        columns = slice(first, first + total.shape[1])
        out_ref[:, columns] = (residual_ref[:, columns].astype(f32) + total).astype(bf16)


def last(residual, left, right):
    return pl.pallas_call(
        last_kernel,
        out_shape=jax.ShapeDtypeStruct(residual.shape, bf16),
        compiler_params=params(2),
        cost_estimate=cost(8 * residual.size, 12 * residual.size),
    )(residual, *left, *right)


def scale_kernel(up_ref, peak_ref, out_ref):
    row = lax.broadcasted_iota(jnp.int32, (SHARE, 128), 0)
    lane = lax.broadcasted_iota(jnp.int32, (SHARE, 128), 1)
    column = jnp.sum(jnp.where(row == lane, peak_ref[...], 0.0), axis=1, keepdims=True)
    out_ref[...] = (up_ref[...] / (column + peak_eps)).astype(bf16)


def scale(up, peak):
    return pl.pallas_call(
        scale_kernel,
        out_shape=jax.ShapeDtypeStruct(up.shape, bf16),
        compiler_params=params(2),
        cost_estimate=cost(4 * up.size, 6 * up.size),
    )(up, peak)


def brought(shift, blocks):
    return [blocks[0]] + [shift(blocks[by], by) for by in range(1, RING)]


def added(shift, blocks):
    return sum((block.astype(f32) for block in brought(shift, blocks)[1:]), blocks[0].astype(f32))


def shards(residual, ln_gain, w_query, w_keyval, w_out, w_up, k_cache, v_cache, lengths):
    narrow, wide = lax.axis_index("narrow"), lax.axis_index("wide")
    place = jnp.stack([narrow >> 1, narrow & 1, wide >> 2, wide & 3]).astype(jnp.int32)
    residual_f32 = residual.astype(f32)
    sums = jnp.stack([jnp.sum(residual_f32, axis=1), jnp.sum(residual_f32 * residual_f32, axis=1)])
    sums = lax.all_to_all(jnp.broadcast_to(sums[None], (NARROW,) + sums.shape), "narrow", 0, 0, tiled=True)
    sums = jnp.sum(sums, axis=0)
    mean = sums[0] / D
    variance = sums[1] / D - mean * mean
    normed = (
        (residual_f32 - mean[:, None]) * lax.rsqrt(variance + norm_eps)[:, None] * ln_gain[None, :]
    ).astype(bf16)
    left, right = gathered(normed)

    keep, send, rows = head_terms(place, left, right, w_query, w_keyval)
    both = keep + swap_core(send)
    rows, both = lax.optimization_barrier((rows, both))
    query = added(shift_z, [both[by] for by in range(RING)]).astype(bf16)
    up_keep, up_send = up_terms(rows, w_up)
    query, up_keep, up_send = lax.optimization_barrier((query, up_keep, up_send))

    query = spread(query.reshape(WIDE, EACH, HCOLS)).reshape(WIDE, RING, EACH, HCOLS)
    query = query.transpose(1, 0, 2, 3).reshape(RING, SHARE, HCOLS)
    other = swap_core(query)
    keep = attend(False, place, lengths, query, k_cache, v_cache)
    send = attend(True, place, lengths, other, k_cache, v_cache)
    send, up_send = lax.optimization_barrier((send, up_send))
    part, up, *blocks = pair(keep, swap_core(send), up_keep, swap_core(up_send))
    blocks = [shift_z(block, by + 1) for by, block in enumerate(blocks)]
    attended, up = finish(place, query, part, up, blocks)

    own = spread(attended.reshape(WIDE, EACH + 1, QCOLS)).reshape(WIDE * RING * (EACH + 1), QCOLS)
    peak, *terms = out_terms(place, own, swap_core(own), w_out)
    left = middle(brought(shift_x, terms[:RING]))
    right = middle(brought(shift_y, terms[RING:]))
    mixed = last(residual, brought(shift_y, left), brought(shift_x, right))
    return (mixed, scale(up, peak), peak[0, :SHARE])


def solution(mesh):
    placed = (
        P("wide", "narrow"),
        P("narrow"),
        P("narrow", "wide"),
        P("narrow", "wide"),
        P("wide", "narrow"),
        P("narrow", "wide"),
        P("wide", "narrow", None),
        P("wide", "narrow", None),
        P("wide"),
    )
    return jax.shard_map(
        shards,
        mesh=mesh,
        in_specs=placed,
        out_specs=(P("wide", "narrow"), P("narrow", "wide"), P("narrow")),
        check_vma=False,
    )
```

```python
import functools

import jax
import jax.numpy as jnp
from jax import lax
from jax.experimental import pallas as pl
from jax.experimental.pallas import tpu as pltpu
from jax.sharding import PartitionSpec as P

D = 18432
HEADS = 48
HEAD = 256
WIDE = 16
NARROW = 8
RING = 4
ROWS = 384
LOCAL = ROWS // WIDE
EACH = LOCAL // NARROW
QCOLS = HEADS * HEAD // WIDE
HELD = QCOLS // HEAD
KVCOLS = 2 * HEAD // WIDE
HCOLS = QCOLS + 128
PACK = EACH * HEAD + 128
FEATS = D // NARROW
SHARE = ROWS // NARROW
UPCOLS = 36864 // WIDE
GATHERED = 1280
SUMMED = 1152
SPAN = RING * LOCAL
UP_PIECES = (256, 1024, 1024)

norm_eps = 1e-05
peak_eps = 1e-06

f32, bf16 = jnp.float32, jnp.bfloat16
SAME_CORE = [[w * NARROW + z * 2 + c for w in range(WIDE) for z in range(RING)] for c in range(2)]


def swap_core(x):
    return lax.ppermute(x, "narrow", [(i, i ^ 1) for i in range(NARROW)])


def shift_z(x, by):
    return lax.ppermute(x, "narrow", [(i, ((i // 2 + by) % RING) * 2 + i % 2) for i in range(NARROW)])


def shift_x(x, by):
    return lax.ppermute(x, "wide", [(i, ((i // RING + by) % RING) * RING + i % RING) for i in range(WIDE)])


def shift_y(x, by):
    return lax.ppermute(x, "wide", [(i, (i // RING) * RING + (i + by) % RING) for i in range(WIDE)])


def gathered(normed):
    left, right = normed[:, :GATHERED], normed[:, GATHERED:]
    left = jnp.concatenate([left] + [shift_x(left, by) for by in range(1, RING)])
    right = jnp.concatenate([right] + [shift_y(right, by) for by in range(1, RING)])
    return (
        [left] + [shift_y(left, by) for by in range(1, RING)],
        [right] + [shift_x(right, by) for by in range(1, RING)],
    )


def spread(x):
    x = jnp.broadcast_to(x[:, None], (WIDE, RING) + x.shape[1:]).reshape((WIDE * RING,) + x.shape[1:])
    return lax.all_to_all(x, ("wide", "narrow"), 0, 0, axis_index_groups=SAME_CORE, tiled=True)


def dot(a, b):
    return jnp.dot(a, b, preferred_element_type=f32)


def full(shape):
    return pl.BlockSpec(shape, lambda *_: (0,) * len(shape))


def params(mib):
    return pltpu.CompilerParams(vmem_limit_bytes=mib * 1024 * 1024)


def cost(flops, moved):
    return pl.CostEstimate(flops=int(flops), bytes_accessed=int(moved), transcendentals=0)


WHOLE = pl.BlockSpec(memory_space=pltpu.VMEM)
HBM = pl.BlockSpec(memory_space=pltpu.HBM)


def slot_of(wide, z, c):
    to_z, to_c = lax.rem((wide >> 2) - z + RING, RING), (wide >> 1) & 1
    return ((to_c ^ c) * RING + to_z) * 2 + (wide & 1)


def held_in(slot, z, c):
    to_z, to_c = lax.rem((slot >> 1) % RING + z, RING), (slot >> 3) ^ c
    return (to_z * 2 + to_c) * 2 + (slot & 1)


def head_kernel(place, *refs):
    left, right = refs[:RING], refs[RING : 2 * RING]
    wq_ref, wkv_ref, keep_ref, send_ref, x_ref, acc_ref, rows_ref = refs[2 * RING :]
    z, c, x, y = place[0], place[1], place[2], place[3]
    for outer in range(RING):
        for first, ref in ((0, left[outer]), (GATHERED, right[outer])):
            held = ref[...].astype(f32)
            for inner in range(RING):
                by_x, by_y = (inner, outer) if first == 0 else (outer, inner)
                source = lax.rem(x - by_x + RING, RING) * RING + lax.rem(y - by_y + RING, RING)
                at = pl.ds(pl.multiple_of(slot_of(source, z, c) * LOCAL, 8), LOCAL)
                rows_ref[at, first : first + held.shape[1]] = held[inner * LOCAL : (inner + 1) * LOCAL]
    x_ref[...] = rows_ref[...].astype(bf16)

    def deal(terms, first):
        for at in range(WIDE):
            rows = pl.ds(pl.multiple_of(held_in(at, z, c) * LOCAL, 8), LOCAL)
            for lanes in range(terms.shape[1] // 128):
                acc_ref[lanes, rows, :] = terms[at * LOCAL : (at + 1) * LOCAL, lanes * 128 : (lanes + 1) * 128]
        for at in range(RING):
            n = lax.rem(z + at, RING) * 2
            for lanes in range(terms.shape[1] // 128):
                columns = slice(first + lanes * 128, first + (lanes + 1) * 128)
                keep_ref[at, :, columns] = acc_ref[lanes, pl.ds(n + c, SHARE, stride=NARROW), :]
                send_ref[at, :, columns] = acc_ref[lanes, pl.ds(n + 1 - c, SHARE, stride=NARROW), :]

    deal(dot(x_ref[...], wq_ref[...]), 0)
    deal(jnp.concatenate([dot(x_ref[...], wkv_ref[...]), jnp.zeros((ROWS, 128 - KVCOLS), f32)], axis=1), QCOLS)


def head_terms(place, left, right, w_query, w_keyval):
    out = jax.ShapeDtypeStruct((RING, SHARE, HCOLS), f32)
    rows = jax.ShapeDtypeStruct((ROWS, FEATS), bf16)
    return pl.pallas_call(
        head_kernel,
        grid_spec=pltpu.PrefetchScalarGridSpec(
            num_scalar_prefetch=1,
            grid=(1,),
            in_specs=[WHOLE] * (2 * RING + 2),
            out_specs=[WHOLE] * 3,
            scratch_shapes=[pltpu.VMEM((QCOLS // 128, ROWS, 128), f32), pltpu.VMEM((ROWS, FEATS), f32)],
        ),
        out_shape=[out, out, rows],
        compiler_params=params(8),
        cost_estimate=cost(2 * ROWS * FEATS * (QCOLS + KVCOLS), 2 * FEATS * (ROWS + QCOLS + 128) + 8 * out.size),
    )(place, *left, *right, w_query, w_keyval)


def up_kernel(x_ref, weights_ref, keep_ref, send_ref, w_ref, sum_ref, sem):
    half, tile = ROWS // 2, 768
    copies, spans, at = [], [], 0
    for count in UP_PIECES:
        span = slice(at, at + count)
        copies.append(pltpu.make_async_copy(weights_ref.at[span], w_ref.at[span], sem.at[len(spans)]))
        spans.append(span)
        at += count
    for copy in copies:
        copy.start()
    for piece, (copy, span) in enumerate(zip(copies, spans)):
        copy.wait()
        for first in range(0, UPCOLS, tile):
            columns = slice(first, first + tile)
            terms = dot(x_ref[:, span], w_ref[span, columns])
            if piece:
                terms += sum_ref[:, columns]
            if piece + 1 < len(spans):
                sum_ref[:, columns] = terms
                continue
            terms = terms.astype(bf16)
            for at in range(RING):
                keep_ref[at, :, columns] = terms[at * SHARE : (at + 1) * SHARE]
                send_ref[at, :, columns] = terms[half + at * SHARE : half + (at + 1) * SHARE]


def up_terms(x, w_up):
    out = jax.ShapeDtypeStruct((RING, SHARE, UPCOLS), bf16)
    return pl.pallas_call(
        up_kernel,
        in_specs=[WHOLE, HBM],
        out_specs=[WHOLE] * 2,
        out_shape=[out, out],
        scratch_shapes=[
            pltpu.VMEM(w_up.shape, bf16),
            pltpu.VMEM((ROWS, UPCOLS), f32),
            pltpu.SemaphoreType.DMA((len(UP_PIECES),)),
        ],
        compiler_params=params(48),
        cost_estimate=cost(2 * ROWS * FEATS * UPCOLS, 2 * (FEATS * (ROWS + UPCOLS) + ROWS * UPCOLS)),
    )(x, w_up)


def parts(value):
    high = value.astype(bf16).astype(f32)
    rest = value - high
    middle = rest.astype(bf16).astype(f32)
    return high, middle, (rest - middle).astype(bf16).astype(f32)


def packed(tops, totals):
    lane = lax.broadcasted_iota(jnp.int32, (tops[0].shape[0], 128), 1)
    out = jnp.zeros(lane.shape, f32)
    for j, (top, total) in enumerate(zip(tops, totals)):
        for at, part in enumerate(parts(top) + parts(total)):
            out = jnp.where(lane == 6 * j + at, part, out)
    return out.astype(bf16)


def unpacked(block, j):
    held = block[:, EACH * HEAD : PACK].astype(f32)
    lanes = [held[:, 6 * j + at : 6 * j + at + 1] for at in range(6)]
    return block[:, j * HEAD : (j + 1) * HEAD].astype(f32), lanes[0] + lanes[1] + lanes[2], lanes[3] + lanes[4] + lanes[5]


def chosen(rows, columns, source):
    made = lax.broadcasted_iota(jnp.int32, (rows, columns), 0)
    held = lax.broadcasted_iota(jnp.int32, (rows, columns), 1)
    return jnp.where(source(made) == held, 1.0, 0.0).astype(bf16)


def by_row(block):
    return dot(chosen(SHARE, SHARE, lambda i: lax.rem(i, WIDE) * EACH + i // WIDE), block)


def heads_of(rows):
    return jnp.concatenate([rows[:, h * HEAD : (h + 1) * HEAD] for h in range(HELD)], axis=0)


def attend_kernel(away, place, lengths, q_ref, keys_ref, values_ref, out_ref, k_ref, v_ref, sem):
    groups = [group_of(away, step, place) for step in range(RING)]
    copies = [
        [pltpu.make_async_copy(source.at[:, group], held.at[step], sem.at[at, step]) for step, group in enumerate(groups)]
        for at, (source, held) in enumerate(((keys_ref, k_ref), (values_ref, v_ref)))
    ]
    for copy in copies[0] + copies[1]:
        copy.start()
    positions = k_ref.shape[2]
    start = (place[0] * 2 + place[1]) * positions
    position = lax.broadcasted_iota(jnp.int32, (HEADS, positions), 1) + start
    rows = [by_row(q_ref[lax.rem(place[0] + step, RING)]) for step in range(RING)]
    for copy in copies[0]:
        copy.wait()
    weights = []
    for step, group in enumerate(groups):
        valid = jnp.concatenate([position < lengths[j * NARROW + group] for j in range(EACH)], axis=0)
        scores = jnp.concatenate(
            [
                lax.dot_general(
                    heads_of(rows[step][j * WIDE : (j + 1) * WIDE]).astype(bf16),
                    k_ref[step, j],
                    (((1,), (1,)), ((), ())),
                    preferred_element_type=f32,
                )
                for j in range(EACH)
            ],
            axis=0,
        )
        masked = jnp.where(valid, scores * (1.0 / HEAD**0.5), f32(-1e30))
        top = jnp.max(masked, axis=1, keepdims=True)
        probs = jnp.where(valid, jnp.exp(masked - top), f32(0.0))
        total = jnp.sum(probs, axis=1, keepdims=True)
        spans = [slice(j * HEADS, (j + 1) * HEADS) for j in range(EACH)]
        out_ref[step, :, EACH * HEAD :] = packed([top[span] for span in spans], [total[span] for span in spans])
        weights.append(probs.astype(bf16))
    for copy in copies[1]:
        copy.wait()
    for step in range(RING):
        for j in range(EACH):
            span = slice(j * HEADS, (j + 1) * HEADS)
            out_ref[step, :, j * HEAD : (j + 1) * HEAD] = dot(weights[step][span], v_ref[step, j]).astype(bf16)


def group_of(away, step, place):
    at = lax.rem(place[0] + step, RING) * 2
    return at + (1 - place[1] if away else place[1])


def attend(away, place, lengths, query, k_cache, v_cache):
    positions = k_cache.shape[1]
    k_cache = k_cache.reshape(EACH, NARROW, positions, HEAD)
    v_cache = v_cache.reshape(EACH, NARROW, positions, HEAD)
    out = jax.ShapeDtypeStruct((RING, HEADS, PACK), bf16)
    return pl.pallas_call(
        functools.partial(attend_kernel, away),
        grid_spec=pltpu.PrefetchScalarGridSpec(
            num_scalar_prefetch=2,
            grid=(1,),
            in_specs=[WHOLE, HBM, HBM],
            out_specs=WHOLE,
            scratch_shapes=[pltpu.VMEM((RING, EACH, positions, HEAD), bf16)] * 2 + [pltpu.SemaphoreType.DMA((2, RING))],
        ),
        out_shape=out,
        compiler_params=params(53),
        cost_estimate=cost(2 * LOCAL * HEADS * positions * HEAD, 2 * k_cache.size + 2 * out.size + 2 * query.size),
    )(place, lengths, query, k_cache, v_cache)


def joined(first, second):
    value_a, top_a, total_a = first
    value_b, top_b, total_b = second
    both = jnp.maximum(top_a, top_b)
    keep_a = jnp.exp(top_a - both)
    keep_b = jnp.exp(top_b - both)
    return value_a * keep_a + value_b * keep_b, both, total_a * keep_a + total_b * keep_b


def pair_kernel(a_ref, b_ref, up_a_ref, up_b_ref, own_ref, up_ref, *send_refs):
    for at in range(RING):
        made = [joined(unpacked(a_ref[at], j), unpacked(b_ref[at], j)) for j in range(EACH)]
        block = jnp.concatenate(
            [value.astype(bf16) for value, _, _ in made] + [packed([top for _, top, _ in made], [total for _, _, total in made])],
            axis=1,
        )
        up = up_a_ref[at].astype(f32) + up_b_ref[at].astype(f32)
        if at == 0:
            own_ref[...] = block
            up_ref[...] = up
        else:
            ref = send_refs[at - 1]
            ref[:, :PACK] = block
            ref[:, PACK:] = up.astype(bf16)


def pair(a, b, up_a, up_b):
    out = [jax.ShapeDtypeStruct(a.shape[1:], bf16), jax.ShapeDtypeStruct(up_a.shape[1:], f32)]
    out += [jax.ShapeDtypeStruct((SHARE, PACK + UPCOLS), bf16)] * (RING - 1)
    return pl.pallas_call(
        pair_kernel,
        out_shape=out,
        compiler_params=params(3),
        cost_estimate=cost(4 * a.size, 6 * a.size + 6 * up_a.size),
    )(a, b, up_a, up_b)


def row_of(block):
    spot = lax.broadcasted_iota(jnp.int32, (KVCOLS, HEAD), 0)
    lane = lax.broadcasted_iota(jnp.int32, (KVCOLS, HEAD), 1)
    tiled = dot(block, (lax.rem(lane, KVCOLS) == spot).astype(bf16))
    row = lax.broadcasted_iota(jnp.int32, tiled.shape, 0)
    lane = lax.broadcasted_iota(jnp.int32, tiled.shape, 1)
    return jnp.sum(jnp.where(lane // KVCOLS == row, tiled, 0.0), axis=0, keepdims=True)


def finish_kernel(place, q_ref, own_ref, up_own_ref, *refs):
    blocks, (out_ref, up_ref) = refs[: RING - 1], refs[RING - 1 :]
    up = sum((ref[:, PACK:].astype(f32) for ref in blocks), up_own_ref[...])
    up_ref[...] = up
    rows = by_row(q_ref[place[0]])
    made = []
    for j in range(EACH):
        mine = rows[j * WIDE : (j + 1) * WIDE]
        query = heads_of(mine)
        keyval = mine[:, QCOLS : QCOLS + KVCOLS].astype(bf16)
        new_key = row_of(keyval[: WIDE // 2])
        new_value = row_of(keyval[WIDE // 2 :])
        own = jnp.sum(query * new_key, axis=1, keepdims=True) * (1.0 / HEAD**0.5)
        value, top, total = functools.reduce(joined, [unpacked(ref, j) for ref in (own_ref, *blocks)])
        both = jnp.maximum(top, own)
        keep = jnp.exp(top - both)
        fresh = jnp.exp(own - both)
        mass = total * keep + fresh
        done = ((value * keep + fresh.astype(bf16).astype(f32) * new_value) / mass).astype(bf16)
        made.append(jnp.concatenate([done[h * WIDE : (h + 1) * WIDE] for h in range(HELD)], axis=1))
    each = EACH + 1
    order = chosen(WIDE * each, SHARE, lambda i: jnp.where(lax.rem(i, each) < EACH, lax.rem(i, each) * WIDE + i // each, -1))
    made = dot(order, jnp.concatenate(made, axis=0))
    column = jnp.max(jnp.abs(up), axis=1, keepdims=True)
    row = lax.broadcasted_iota(jnp.int32, (SHARE, 128), 0)
    lane = lax.broadcasted_iota(jnp.int32, (SHARE, 128), 1)
    peak = jnp.sum(jnp.where(row == lane, column, 0.0), axis=0, keepdims=True)
    peaks = jnp.concatenate(parts(peak) + (jnp.zeros((1, QCOLS - 3 * 128), f32),), axis=1)
    row = lax.broadcasted_iota(jnp.int32, made.shape, 0)
    out_ref[...] = jnp.where(lax.rem(row, each) == EACH, peaks, made).astype(bf16)


def finish(place, query, own, up_own, blocks):
    out = [
        jax.ShapeDtypeStruct((WIDE * (EACH + 1), QCOLS), bf16),
        jax.ShapeDtypeStruct(up_own.shape, f32),
    ]
    return pl.pallas_call(
        finish_kernel,
        grid_spec=pltpu.PrefetchScalarGridSpec(
            num_scalar_prefetch=1,
            grid=(1,),
            in_specs=[WHOLE] * (len(blocks) + 3),
            out_specs=[WHOLE] * 2,
        ),
        out_shape=out,
        compiler_params=params(3),
        cost_estimate=cost(40 * own.size, 10 * own.size + 14 * up_own.size),
    )(place, query, own, up_own, *blocks)


def out_kernel(place, own_ref, other_ref, w_ref, peak_ref, *out_refs):
    each = EACH + 1
    shape = (ROWS, own_ref.shape[0])
    made = lax.broadcasted_iota(jnp.int32, shape, 0)
    held = lax.broadcasted_iota(jnp.int32, shape, 1)
    at, local = made // LOCAL, lax.rem(made, LOCAL)
    group = lax.rem(local, NARROW)
    for along_x in (True, False):
        outer, inner = at // RING, lax.rem(at, RING)
        by_x, by_y = (outer, inner) if along_x else (inner, outer)
        wide = lax.rem(place[2] + by_x, RING) * RING + lax.rem(place[3] + by_y, RING)
        source = (wide * RING + group // 2) * each + local // NARROW
        rows = jnp.zeros((ROWS, QCOLS), f32)
        for core, ref in ((place[1], own_ref), (1 - place[1], other_ref)):
            pick = jnp.where(source == held, jnp.where(lax.rem(group, 2) == core, 1.0, 0.0), 0.0)
            rows += dot(pick.astype(bf16), ref[...])
        rows = rows.astype(bf16)
        refs = out_refs[:RING] if along_x else out_refs[RING:]
        start, width = (0, SUMMED) if along_x else (SUMMED, FEATS - SUMMED)
        for first in range(0, width, 1152):
            terms = dot(rows, w_ref[:, start + first : start + first + 1152]).astype(bf16)
            for slot, ref in enumerate(refs):
                ref[:, first : first + 1152] = terms[slot * SPAN : (slot + 1) * SPAN]
    peaks = own_ref[...].astype(f32)
    peaks = peaks[:, 0:128] + peaks[:, 128:256] + peaks[:, 256:384]
    row = lax.broadcasted_iota(jnp.int32, peaks.shape, 0)
    mine = jnp.where(lax.rem(row, each) == EACH, lax.rem(row // each, RING), -1) == place[0]
    peak_ref[...] = jnp.max(jnp.where(mine, peaks, 0.0), axis=0, keepdims=True)


def out_terms(place, own, other, w_out):
    return pl.pallas_call(
        out_kernel,
        grid_spec=pltpu.PrefetchScalarGridSpec(
            num_scalar_prefetch=1,
            grid=(1,),
            in_specs=[WHOLE] * 3,
            out_specs=[WHOLE] * (1 + 2 * RING),
        ),
        out_shape=[jax.ShapeDtypeStruct((1, 128), f32)]
        + [jax.ShapeDtypeStruct((SPAN, SUMMED), bf16)] * RING
        + [jax.ShapeDtypeStruct((SPAN, FEATS - SUMMED), bf16)] * RING,
        compiler_params=params(6),
        cost_estimate=cost(2 * ROWS * QCOLS * FEATS, 2 * (QCOLS * FEATS + ROWS * FEATS)),
    )(place, own, other, w_out)


def middle_kernel(*refs):
    blocks, (own_ref, *send_refs) = refs[:RING], refs[RING:]
    total = sum((ref[...].astype(f32) for ref in blocks[1:]), blocks[0][...].astype(f32))
    own_ref[...] = total[:LOCAL]
    for at, ref in enumerate(send_refs):
        ref[...] = total[(at + 1) * LOCAL : (at + 2) * LOCAL].astype(bf16)


def middle(blocks):
    width = blocks[0].shape[1]
    return pl.pallas_call(
        middle_kernel,
        out_shape=[jax.ShapeDtypeStruct((LOCAL, width), f32)] + [jax.ShapeDtypeStruct((LOCAL, width), bf16)] * (RING - 1),
        compiler_params=params(4),
        cost_estimate=cost(4 * blocks[0].size, 12 * blocks[0].size),
    )(*blocks)


def last_kernel(residual_ref, *refs):
    left, right, out_ref = refs[:RING], refs[RING : 2 * RING], refs[2 * RING]
    for first, blocks in ((0, left), (SUMMED, right)):
        total = sum((ref[...].astype(f32) for ref in blocks[1:]), blocks[0][...])
        columns = slice(first, first + total.shape[1])
        out_ref[:, columns] = (residual_ref[:, columns].astype(f32) + total).astype(bf16)


def last(residual, left, right):
    return pl.pallas_call(
        last_kernel,
        out_shape=jax.ShapeDtypeStruct(residual.shape, bf16),
        compiler_params=params(2),
        cost_estimate=cost(8 * residual.size, 12 * residual.size),
    )(residual, *left, *right)


def scale_kernel(up_ref, peak_ref, out_ref):
    row = lax.broadcasted_iota(jnp.int32, (SHARE, 128), 0)
    lane = lax.broadcasted_iota(jnp.int32, (SHARE, 128), 1)
    column = jnp.sum(jnp.where(row == lane, peak_ref[...], 0.0), axis=1, keepdims=True)
    out_ref[...] = (up_ref[...] / (column + peak_eps)).astype(bf16)


def scale(up, peak):
    return pl.pallas_call(
        scale_kernel,
        out_shape=jax.ShapeDtypeStruct(up.shape, bf16),
        compiler_params=params(2),
        cost_estimate=cost(4 * up.size, 6 * up.size),
    )(up, peak)


def brought(shift, blocks):
    return [blocks[0]] + [shift(blocks[by], by) for by in range(1, RING)]


def added(shift, blocks):
    return sum((block.astype(f32) for block in brought(shift, blocks)[1:]), blocks[0].astype(f32))


def shards(residual, ln_gain, w_query, w_keyval, w_out, w_up, k_cache, v_cache, lengths):
    narrow, wide = lax.axis_index("narrow"), lax.axis_index("wide")
    place = jnp.stack([narrow >> 1, narrow & 1, wide >> 2, wide & 3]).astype(jnp.int32)
    residual_f32 = residual.astype(f32)
    sums = jnp.stack([jnp.sum(residual_f32, axis=1), jnp.sum(residual_f32 * residual_f32, axis=1)])
    sums = lax.all_to_all(jnp.broadcast_to(sums[None], (NARROW,) + sums.shape), "narrow", 0, 0, tiled=True)
    sums = jnp.sum(sums, axis=0)
    mean = sums[0] / D
    variance = sums[1] / D - mean * mean
    normed = (
        (residual_f32 - mean[:, None]) * lax.rsqrt(variance + norm_eps)[:, None] * ln_gain[None, :]
    ).astype(bf16)
    left, right = gathered(normed)

    keep, send, rows = head_terms(place, left, right, w_query, w_keyval)
    both = keep + swap_core(send)
    rows, both = lax.optimization_barrier((rows, both))
    query = added(shift_z, [both[by] for by in range(RING)]).astype(bf16)
    up_keep, up_send = up_terms(rows, w_up)
    query, up_keep, up_send = lax.optimization_barrier((query, up_keep, up_send))

    query = spread(query.reshape(WIDE, EACH, HCOLS)).reshape(WIDE, RING, EACH, HCOLS)
    query = query.transpose(1, 0, 2, 3).reshape(RING, SHARE, HCOLS)
    other = swap_core(query)
    keep = attend(False, place, lengths, query, k_cache, v_cache)
    send = attend(True, place, lengths, other, k_cache, v_cache)
    send, up_send = lax.optimization_barrier((send, up_send))
    part, up, *blocks = pair(keep, swap_core(send), up_keep, swap_core(up_send))
    blocks = [shift_z(block, by + 1) for by, block in enumerate(blocks)]
    attended, up = finish(place, query, part, up, blocks)

    own = spread(attended.reshape(WIDE, EACH + 1, QCOLS)).reshape(WIDE * RING * (EACH + 1), QCOLS)
    peak, *terms = out_terms(place, own, swap_core(own), w_out)
    left = middle(brought(shift_x, terms[:RING]))
    right = middle(brought(shift_y, terms[RING:]))
    mixed = last(residual, brought(shift_y, left), brought(shift_x, right))
    return (mixed, scale(up, peak), peak[0, :SHARE])


def solution(mesh):
    placed = (
        P("wide", "narrow"),
        P("narrow"),
        P("narrow", "wide"),
        P("narrow", "wide"),
        P("wide", "narrow"),
        P("narrow", "wide"),
        P("wide", "narrow", None),
        P("wide", "narrow", None),
        P("wide"),
    )
    return jax.shard_map(
        shards,
        mesh=mesh,
        in_specs=placed,
        out_specs=(P("wide", "narrow"), P("narrow", "wide"), P("narrow")),
        check_vma=False,
    )
```
